512 devices in a mesh: dp: 64 (over y, z_lo, x), head: 8 (over z_hi, core).
Axes of the slice: x: 4, y: 8, z: 8 (z_hi: 4, z_lo: 2; z = z_hi * 2 + z_lo), core: 2. Of those that a mesh axis runs over, the one named last changes fastest.
Arguments:
- queries: bfloat16 [8192, 16384], P('dp', 'head'), may hold values from -100 to 100
- tree_keys: bfloat16 [8192, 1024], P('dp', 'head'), may hold values from -4 to 4
- tree_values: bfloat16 [8192, 1024], P('dp', 'head'), may hold values from -4 to 4
- cache_keys: bfloat16 [512, 128, 1024], P('dp', None, 'head'), may hold values from -4 to 4
- cache_values: bfloat16 [512, 128, 1024], P('dp', None, 'head'), may hold values from -4 to 4
- parents: int32 [512, 16], P('dp'), may hold values from -1 to 14, as said below
- cache_lengths: int32 [512], P('dp'), may hold values from 16 to 128, as said below
- accepted_counts: int32 [512], P('dp'), may hold values from 4 to 16, as said below
- dest_map: int32 [8192, 1], P('dp'), may hold values from 0 to 63; in each aligned block of 128 rows (0 to 127, 128 to 255, ...) at most 3 rows name the same one
- low_hidden: bfloat16 [8192, 16384], P('dp', 'head'), may hold values from -320 to 320
- mid_hidden: bfloat16 [8192, 16384], P('dp', 'head'), may hold values from -320 to 320
- norm_gains: bfloat16 [3, 16384], P(None, 'head'), may hold values from 0.099609375 to 1.8984375
- merge_down: bfloat16 [16384, 384], P('head'), may hold values from -0.02734375 to 0.02734375
- merge_up: bfloat16 [128, 16384], P(None, 'head'), may hold values from -0.5 to 0.5
- out_grad: bfloat16 [12288, 16384], P('dp', 'head'), may hold values from -0.059814453 to 0.059814453
Outputs:
- gradient_merge_down: float32 [16384, 384], P('head')
- grad_up: float32 [128, 16384], P(None, 'head')
The draws below stay inside these ranges and needn't reach their ends.
Inputs may be any that keep to these rules, and one draw needn't show every extreme that they name: parents[b, 0] = -1, and 0 <= parents[b, t] < t for t >= 1. `cache_lengths`: some branch has all 128 positions live. A branch accepts its first accepted_counts[b] tree tokens; some branch accepts all 16. `dest_map`: among the rows of one dp index, each trainer shard is named at most 3 times.
All inputs are finite; a program needn't handle non-finite values.
Results may differ from the reference program's by a relative error of at most 0.0055.
Values may be sent and summed in bfloat16 or wider, within the bound.
No kernel may reach another device: no remote copies, remote signals or barrier semaphores. Data moves between devices by JAX's collectives and lax.ppermute only.
A program may use at most 64 MiB of HBM per device.

```python
import math
import jax
import jax.numpy as jnp
import numpy as np
from jax import lax

MODEL_WIDTH = 16384
QHEADS = 128
KVHEADS = 8
HEAD_DIM = 128
INNER_RANK = 128
TREE = 16
BR_DEV = 8
CACHE = 128
BRANCHES = 512
ROWS = 8192
ROWS_DEV = 128
MOST = 3
ALL_SLOTS = 12288
N_DP = 64


def drawn_pair(key):
    keys_raw = jnp.clip(jax.random.normal(jax.random.fold_in(key, 11), (BRANCHES, CACHE, KVHEADS, HEAD_DIM), jnp.float32), -4.0, 4.0)
    query_raw = jnp.clip(jax.random.normal(jax.random.fold_in(key, 12), (BRANCHES, TREE, KVHEADS, QHEADS // KVHEADS, HEAD_DIM), jnp.float32), -4.0, 4.0)
    return (keys_raw, query_raw)


def draw_queries(key, part):
    keys_raw, query_raw = drawn_pair(key)
    return query_raw.reshape(BRANCHES * TREE, QHEADS * HEAD_DIM).astype(jnp.bfloat16)


def draw_cache_keys(key, part):
    keys_raw, query_raw = drawn_pair(key)
    return keys_raw.reshape(BRANCHES, CACHE, KVHEADS * HEAD_DIM).astype(jnp.bfloat16)


def hidden_rows(key):
    base = jnp.clip(jax.random.normal(key, (ROWS, MODEL_WIDTH), jnp.float32), -4.0, 4.0)
    column = 3.0 ** (jnp.arange(MODEL_WIDTH, dtype=jnp.float32) / max(MODEL_WIDTH - 1, 1)) * jnp.exp(jax.random.uniform(jax.random.fold_in(key, 1), (MODEL_WIDTH,), jnp.float32, 0.0, 1.2))
    row_scale = jnp.exp(jax.random.uniform(jax.random.fold_in(key, 3), (ROWS, 1), jnp.float32, 0.0, 2.3))
    return base * column[None, :] * row_scale / 3.0


def draw_low_hidden(key, part):
    return hidden_rows(jax.random.fold_in(key, 21)).astype(jnp.bfloat16)


def draw_mid_hidden(key, part):
    return hidden_rows(jax.random.fold_in(key, 22)).astype(jnp.bfloat16)


def draw_cache_lengths(key, part):
    shortest = max(2, CACHE // 8)
    lengths = jax.random.randint(key, (BRANCHES,), shortest, CACHE + 1)
    chosen = jax.random.randint(jax.random.fold_in(key, 1), (), 0, BRANCHES)
    return lengths.at[chosen].set(CACHE).astype(jnp.int32)


def draw_accepted_counts(key, part):
    fewest = max(1, TREE // 4)
    counts = jax.random.randint(key, (BRANCHES,), fewest, TREE + 1)
    chosen = jax.random.randint(jax.random.fold_in(key, 1), (), 0, BRANCHES)
    return counts.at[chosen].set(TREE).astype(jnp.int32)


def draw_parents(key, part):
    raw_draw = jax.random.randint(key, (BRANCHES, TREE), 0, 1 << 20)
    positions = jnp.arange(TREE)[None, :]
    linked = jnp.where(positions == 0, -1, raw_draw % jnp.maximum(positions, 1))
    chosen = jax.random.randint(jax.random.fold_in(key, 1), (), 0, BRANCHES)
    return linked.at[chosen, TREE - 1].set(TREE - 2).astype(jnp.int32)


def levels(rng, extent, cuts, low, high):
    factor_of, own = 1.0, jax.random.fold_in(rng, 6)
    for dim, shards_of in cuts:
        heights = jnp.exp(jax.random.uniform(jax.random.fold_in(own, dim), (shards_of,), jnp.float32, low / len(cuts), high / len(cuts)))
        factor_of = factor_of * jnp.repeat(heights, extent[dim] // shards_of).reshape([-1 if axis == dim else 1 for axis in range(len(extent))])
    return factor_of


def shared_out(key, own, number, rows, count, top, bound, lean):
    sequence = jax.random.permutation(key, count)
    packed, usual = load_shares(count, rows * top, bound, lean, True), load_shares(count, rows * top, bound, lean, False)
    places = jnp.arange(count)

    def named(sizes, offset_by):
        used = int((sizes > 0).sum())
        fixed = max(1, used // 4)
        passed = fixed + (places - fixed + offset_by * (used - fixed)) % max(1, count - fixed)
        return jnp.zeros((count,), jnp.int32).at[sequence[jnp.where(places < fixed, places, passed)]].set(jnp.asarray(sizes, jnp.int32))

    sizes = jnp.where(number % 4 == 0, named(packed, number // 4), named(usual, number - number // 4 - 1))
    mixed = jax.random.permutation(jax.random.fold_in(own, 3), count)
    giver, receiver = mixed[0:count // 2 * 2:2], mixed[1:count // 2 * 2:2]
    room = jnp.minimum(sizes[giver] - 1, bound - sizes[receiver]) // 2
    room = jnp.where((giver == sequence[0]) | (receiver == sequence[0]) | (sizes[receiver] == 0), 0, jnp.maximum(room, 0))
    passed = jax.random.randint(jax.random.fold_in(own, 4), (count // 2,), 0, 1 << 20) % (room + 1)
    sizes = sizes.at[giver].add(-passed).at[receiver].add(passed)
    labels = jnp.searchsorted(jnp.cumsum(sizes), jnp.arange(rows * top), side="right").astype(jnp.int32)
    listing = labels.reshape(top, rows).T
    listing = listing[jax.random.permutation(jax.random.fold_in(own, 1), rows)]
    offset_by = jax.random.randint(jax.random.fold_in(own, 2), (rows, 1), 0, top)
    return jnp.take_along_axis(listing, (jnp.arange(top)[None, :] + offset_by) % top, axis=1)


def load_shares(count, total, bound, slope, full):
    loads = [(1 << 20) // math.isqrt(standing ** slope) + 1 for standing in range(1, count + 1)]
    largest = bound if full else min(bound, max(-(-total // count), total * loads[0] // sum(loads)))
    least = 1 if total - largest >= count - 1 else 0
    given, spare = [largest] + [least] * (count - 1), total - largest - least * (count - 1)
    while spare > 0:
        free = [i for i in range(1, count) if given[i] < largest] or [i for i in range(1, count) if given[i] < bound]
        mass, left = sum([loads[i] for i in free]), spare
        for i in free:
            more = min(bound - given[i], max(1, left * loads[i] // mass), spare)
            given[i] = given[i] + more
            spare = spare - more
    return np.array(given)


def gaussian(rng, shape, spread, limit, cuts=(), kind=jnp.bfloat16):
    entries = jax.random.normal(rng, shape, jnp.float32) * spread
    if len(cuts) > 0:
        entries = levels(rng, shape, cuts, -0.22, 0.18) * entries
    return jnp.clip(entries, min=-limit, max=limit).astype(kind)


def setup_inputs(seed: int = 0) -> dict:
    streams_of = jax.random.split(jax.random.key(seed), 16)
    queries = draw_queries(jax.random.fold_in(streams_of[15], 71), 0)
    tree_keys = gaussian(streams_of[1], (ROWS, KVHEADS * HEAD_DIM), 1.0, 4.0, ((0, 64), (1, 8)))
    tree_values = gaussian(streams_of[2], (ROWS, KVHEADS * HEAD_DIM), 1.0, 4.0, ((0, 64), (1, 8)))
    cache_keys = draw_cache_keys(jax.random.fold_in(streams_of[15], 71), 0)
    cache_values = gaussian(streams_of[4], (BRANCHES, CACHE, KVHEADS * HEAD_DIM), 1.0, 4.0, ((0, 64), (2, 8)))
    parents = draw_parents(jax.random.fold_in(streams_of[15], 71), 0)
    cache_lengths = draw_cache_lengths(jax.random.fold_in(streams_of[15], 71), 0)
    accepted_counts = draw_accepted_counts(jax.random.fold_in(streams_of[15], 71), 0)
    dest_map_keys = jax.random.split(jax.random.fold_in(streams_of[8], 1), ROWS // ROWS_DEV)
    dest_map_turns = jax.random.permutation(jax.random.fold_in(streams_of[8], 3), ROWS // ROWS_DEV)
    dest_map = jax.vmap(lambda own, number: shared_out(jax.random.fold_in(streams_of[8], 2), own, number, ROWS_DEV, N_DP, 1, MOST, 2))(dest_map_keys, dest_map_turns).reshape((ROWS, 1))
    low_hidden = draw_low_hidden(jax.random.fold_in(streams_of[15], 71), 0)
    mid_hidden = draw_mid_hidden(jax.random.fold_in(streams_of[15], 71), 0)
    norm_gains = jnp.clip(1.0 + 0.18 * jax.random.normal(streams_of[11], (3, MODEL_WIDTH), jnp.float32), 0.099609375, 1.8984375).astype(jnp.bfloat16)
    merge_down = gaussian(streams_of[12], (MODEL_WIDTH, 3 * INNER_RANK), (3 * MODEL_WIDTH) ** -0.5, 0.02734375, ((0, 8),))
    merge_up = gaussian(streams_of[13], (INNER_RANK, MODEL_WIDTH), INNER_RANK ** -0.5, 0.5, ((1, 8),))
    out_grad = gaussian(streams_of[14], (ALL_SLOTS, MODEL_WIDTH), 0.01, 0.059814453, ((0, 64), (1, 8)))
    return {"queries": queries, "tree_keys": tree_keys, "tree_values": tree_values, "cache_keys": cache_keys, "cache_values": cache_values, "parents": parents, "cache_lengths": cache_lengths, "accepted_counts": accepted_counts, "dest_map": dest_map, "low_hidden": low_hidden, "mid_hidden": mid_hidden, "norm_gains": norm_gains, "merge_down": merge_down, "merge_up": merge_up, "out_grad": out_grad}


EPSILON = 1e-05
MASKED = -1e+30

def ancestors(parents):
    positions = jnp.arange(TREE)
    reached = (parents[:, :, None] == positions[None, None, :]).astype(jnp.float32) + jnp.eye(TREE, dtype=jnp.float32)[None]
    for repeat_no in range(max(1, (TREE - 1).bit_length())):
        reached = jnp.minimum(jnp.einsum('nts,nsu->ntu', reached, reached, precision=lax.Precision.HIGHEST), 1.0)
    return reached > 0.5

def verify_attention(queries, tree_keys, tree_values, cache_keys, cache_values, parents, cache_lengths):
    branches = parents.shape[0]
    groups = cache_keys.shape[2] // HEAD_DIM
    group_size = QHEADS // KVHEADS
    cache_len = cache_keys.shape[1]
    score_scale = HEAD_DIM ** (-0.5)
    query_heads = queries.reshape(branches, TREE, groups, group_size, HEAD_DIM).astype(jnp.float32)
    far_keys = cache_keys.reshape(branches, cache_len, groups, HEAD_DIM).astype(jnp.float32)
    far_values = cache_values.reshape(branches, cache_len, groups, HEAD_DIM).astype(jnp.float32)
    near_keys = tree_keys.reshape(branches, TREE, groups, HEAD_DIM).astype(jnp.float32)
    near_values = tree_values.reshape(branches, TREE, groups, HEAD_DIM).astype(jnp.float32)
    cache_scores = jnp.einsum('btgjd,bpgd->bgjtp', query_heads, far_keys) * score_scale
    tree_scores = jnp.einsum('btgjd,bsgd->bgjts', query_heads, near_keys) * score_scale
    visible = jnp.arange(cache_len)[None, :] < cache_lengths[:, None]
    cache_scores = jnp.where(visible[:, None, None, None, :], cache_scores, MASKED)
    tree_scores = jnp.where(ancestors(parents)[:, None, None, :, :], tree_scores, MASKED)
    row_max = jnp.maximum(lax.optimization_barrier(jnp.max(cache_scores, axis=-1)), lax.optimization_barrier(jnp.max(tree_scores, axis=-1)))
    cache_weights = jnp.exp(cache_scores - row_max[..., None])
    tree_weights = jnp.exp(tree_scores - row_max[..., None])
    denominator = lax.optimization_barrier(jnp.sum(cache_weights, axis=-1)) + lax.optimization_barrier(jnp.sum(tree_weights, axis=-1))
    cache_probs = (cache_weights / denominator[..., None]).astype(jnp.bfloat16)
    tree_probs = (tree_weights / denominator[..., None]).astype(jnp.bfloat16)
    attended = jnp.einsum('bgjtp,bpgd->btgjd', cache_probs.astype(jnp.float32), far_values)
    attended = attended + jnp.einsum('bgjts,bsgd->btgjd', tree_probs.astype(jnp.float32), near_values)
    return attended.reshape(branches * TREE, groups * group_size * HEAD_DIM).astype(jnp.bfloat16)

def draft_terms(features, grad_in, norm_gains, merge_down, merge_up):
    widened = features.astype(jnp.float32)
    inverse = lax.rsqrt(lax.optimization_barrier(jnp.mean(widened * widened, axis=2)) + EPSILON)
    rescaled_rows = (widened * norm_gains.astype(jnp.float32)[None]).astype(jnp.bfloat16)
    downward_projection = merge_down.astype(jnp.float32).reshape(MODEL_WIDTH, 3, INNER_RANK)
    partial_terms = jnp.einsum('otd,dtq->otq', rescaled_rows.astype(jnp.float32), downward_projection)
    mixed_rank = lax.optimization_barrier(jnp.sum(inverse[:, :, None] * partial_terms, axis=1))
    active = jax.nn.silu(mixed_rank).astype(jnp.bfloat16)
    back_rows = jnp.dot(grad_in, merge_up.T, preferred_element_type=jnp.float32)
    sigmoid_z = jax.nn.sigmoid(mixed_rank)
    grad_mixed = back_rows * sigmoid_z * (1.0 + mixed_rank * (1.0 - sigmoid_z))
    gradient_rescaled = (inverse[:, :, None] * grad_mixed[:, None, :]).astype(jnp.bfloat16)
    gradient_merge_down = jnp.einsum('qwb,qwk->bwk', rescaled_rows.astype(jnp.float32), gradient_rescaled.astype(jnp.float32)).reshape(MODEL_WIDTH, 3 * INNER_RANK)
    grad_up = jnp.einsum('nr,nc->rc', active.astype(jnp.float32), grad_in.astype(jnp.float32))
    return (gradient_merge_down, grad_up)

def by_source(array):
    return array.reshape((N_DP, array.shape[0] // N_DP) + array.shape[1:])

def reference(queries, tree_keys, tree_values, cache_keys, cache_values, parents, cache_lengths, accepted_counts, dest_map, low_hidden, mid_hidden, norm_gains, merge_down, merge_up, out_grad):
    row_count = BR_DEV * TREE
    stacked = tuple((by_source(array) for array in (queries, tree_keys, tree_values, cache_keys, cache_values, parents, cache_lengths, accepted_counts, dest_map, low_hidden, mid_hidden)))

    def per_source(running, source_item):
        source, pieces = source_item
        query_rows, near_keys, near_values, far_keys, far_values, parent_rows, lengths, counts, targets, low_rows, mid_rows = pieces
        attended = verify_attention(query_rows, near_keys, near_values, far_keys, far_values, parent_rows, lengths)
        accepted = jnp.arange(row_count) % TREE < jnp.repeat(counts, TREE, total_repeat_length=row_count)
        features = jnp.stack([low_rows, mid_rows, attended], axis=1) * accepted[:, None, None].astype(jnp.bfloat16)
        target = targets[:, 0]
        one_hot = (target[:, None] == jnp.arange(N_DP)[None, :]).astype(jnp.float32)
        earlier = (jnp.arange(row_count)[:, None] > jnp.arange(row_count)[None, :]).astype(jnp.float32)
        before = jnp.dot(earlier, one_hot, precision=lax.Precision.HIGHEST)
        slot_rank = lax.optimization_barrier(jnp.sum(before * one_hot, axis=1)).astype(jnp.int32)
        slot_index = (target * (N_DP * MOST) + source * MOST + slot_rank).astype(jnp.int32)
        grad_in = jnp.take(out_grad, slot_index, axis=0)
        gradient_merge_down, grad_up = draft_terms(features, grad_in, norm_gains, merge_down, merge_up)
        return ((running[0] + gradient_merge_down, running[1] + grad_up), None)
    start = (jnp.zeros((MODEL_WIDTH, 3 * INNER_RANK), jnp.float32), jnp.zeros((INNER_RANK, MODEL_WIDTH), jnp.float32))
    totals, unused = lax.scan(per_source, start, (jnp.arange(N_DP, dtype=jnp.int32), stacked))
    return (totals[0], totals[1])
```

```python
import functools

import jax
import jax.numpy as jnp
from jax import lax
from jax.experimental import pallas as pl
from jax.experimental.pallas import tpu as pltpu
from jax.sharding import Mesh, PartitionSpec as P

MODEL_WIDTH = 16384
HEAD_DIM = 128
TREE = 16
CACHE = 128
RANK = 128
MOST = 3
EPSILON = 1e-05
MASKED = -1e30
BF = jnp.bfloat16
F32 = jnp.float32
VMEM_LIMIT = 48 * 1024 * 1024


def params():
    return pltpu.CompilerParams(vmem_limit_bytes=VMEM_LIMIT)


def iota(shape, dim):
    return lax.broadcasted_iota(jnp.int32, shape, dim)


def dot(a, b):
    return jnp.dot(a, b, preferred_element_type=F32)


def dot_nt(a, b):
    return lax.dot_general(a, b, (((1,), (1,)), ((), ())), preferred_element_type=F32)


def dot_tn(a, b):
    return lax.dot_general(a, b, (((0,), (0,)), ((), ())), preferred_element_type=F32)


def feature_kernel(
    lengths,
    counts,
    parents,
    queries,
    tree_keys,
    tree_values,
    cache_keys,
    cache_values,
    low,
    mid,
    gains,
    merge_down,
    turned,
    partial,
    reach,
    rows,
    squares,
):
    branch = pl.program_id(0)
    branches = pl.num_programs(0)
    count, width = rows.shape[1], rows.shape[2]
    heads = width // HEAD_DIM

    @pl.when(branch == 0)
    def _():
        groups = parents.shape[0]
        owner = (iota((count, groups), 0) // TREE == iota((count, groups), 1)).astype(F32)
        spread = jnp.dot(owner, parents[...].astype(F32), preferred_element_type=F32)
        own = iota((count, TREE), 0) % TREE == iota((count, TREE), 1)
        parent = jnp.sum(jnp.where(own, spread, 0.0), axis=1, keepdims=True).astype(jnp.int32)
        row, column = iota((count, count), 0), iota((count, count), 1)
        linked = (column == row) | ((parent >= 0) & (column == row // TREE * TREE + parent))
        reached = jnp.where(linked, 1.0, 0.0)
        for _ in range((TREE - 1).bit_length()):
            step = reached.astype(BF)
            reached = jnp.minimum(dot(step, step), 1.0)
        reach[...] = reached

    start = pl.multiple_of(branch * TREE, TREE)
    here = pl.ds(start, TREE)
    query = queries[...]
    query = jnp.concatenate(
        [query[:, h * HEAD_DIM : (h + 1) * HEAD_DIM] for h in range(heads)], axis=0
    )
    keys = jnp.concatenate([cache_keys[0], tree_keys[...]], axis=0)
    values = jnp.concatenate([cache_values[0], tree_values[...]], axis=0)
    scores = dot_nt(query, keys) * (HEAD_DIM**-0.5)
    live = jnp.where(iota((TREE, CACHE), 1) < lengths[branch], 1.0, 0.0)
    seen = jnp.concatenate([live, reach[here, :]], axis=1) > 0.5
    scores = jnp.where(seen[None], scores.reshape(heads, TREE, CACHE + count), MASKED)
    weights = jnp.exp(scores - jnp.max(scores, axis=2, keepdims=True))
    probs = (weights / jnp.sum(weights, axis=2, keepdims=True)).astype(BF)
    attended = dot(probs.reshape(heads * TREE, CACHE + count), values).astype(BF)
    attended = jnp.concatenate(
        [attended[h * TREE : (h + 1) * TREE, :] for h in range(heads)], axis=1
    )
    kept = iota((TREE, 1), 0) < counts[branch]
    lane = iota((TREE, RANK), 1)
    totals = jnp.zeros((TREE, RANK), F32)
    for layer, feature in enumerate((low[...], mid[...], attended)):
        feature = jnp.where(kept, feature.astype(F32), 0.0)
        total = jnp.sum(feature * feature, axis=1, keepdims=True)
        rough = total.astype(BF).astype(F32)
        totals = totals + jnp.where(lane == layer, rough, 0.0)
        totals = totals + jnp.where(lane == 3 + layer, total - rough, 0.0)
        gain = gains[layer : layer + 1, :].astype(F32)
        rows[layer, here, :] = (feature * gain).astype(BF)
    squares[here, :] = totals.astype(BF)

    @pl.when(branch == branches - 1)
    def _():
        for layer in range(3):
            block = rows[layer]
            columns = slice(layer * RANK, (layer + 1) * RANK)
            partial[:, columns] = dot(block, merge_down[:, columns]).astype(BF)
            turned[layer] = block.T
        partial[:, 3 * RANK :] = squares[...]


def back_kernel(targets, received, merge_up, partial, sent, chosen):
    count, slots = chosen.shape
    peers = slots // MOST
    target = targets[...]
    named = (target == iota((count, peers), 1)).astype(F32)
    earlier = (iota((count, count), 0) > iota((count, count), 1)).astype(BF)
    before = dot(earlier, named.astype(BF))
    place = target * MOST + jnp.sum(before * named, axis=1, keepdims=True).astype(jnp.int32)
    pick = (place == iota((count, slots), 1)).astype(BF)
    back = dot_nt(received[...], merge_up[...]).astype(BF)
    chosen[...] = pick
    sent[:, : 3 * RANK] = partial[:, : 3 * RANK]
    sent[:, 3 * RANK : 4 * RANK] = dot(pick, back).astype(BF)
    sent[:, 4 * RANK :] = partial[:, 3 * RANK :]


def merge_kernel(parts, out):
    total = parts[0].astype(F32)
    for peer in range(1, parts.shape[0]):
        total = total + parts[peer].astype(F32)
    squares = total[:, 4 * RANK :]
    inverse = [
        lax.rsqrt(
            (squares[:, i : i + 1] + squares[:, 3 + i : 4 + i]) / MODEL_WIDTH + EPSILON
        )
        for i in range(3)
    ]
    mixed = inverse[0] * total[:, :RANK]
    for i in (1, 2):
        mixed = mixed + inverse[i] * total[:, i * RANK : (i + 1) * RANK]
    back = total[:, 3 * RANK : 4 * RANK]
    gate = 1.0 / (1.0 + jnp.exp(-mixed))
    grad = back * gate * (1.0 + mixed * (1.0 - gate))
    result = [(inverse[i] * grad).astype(BF) for i in range(3)] + [(mixed * gate).astype(BF)]
    out[...] = jnp.broadcast_to(jnp.concatenate(result, axis=1)[None], out.shape)


def grads_kernel(turned, received, merged, chosen, out, up):
    step = pl.program_id(0)
    width = received.shape[1]

    @pl.when(step == 0)
    def _():
        placed = dot_tn(merged[:, 3 * RANK :], chosen[...]).astype(BF)
        up[...] = dot(placed, received[...]).astype(BF)

    for layer in range(3):
        columns = slice(layer * RANK, (layer + 1) * RANK)
        out[0, :, columns] = dot(turned[layer], merged[:, columns]).astype(BF)
    rows = up.shape[0] // pl.num_programs(0)
    block = up[pl.ds(pl.multiple_of(step * rows, rows), rows), :]
    for j in range(width // RANK):
        out[0, j * rows : (j + 1) * rows, 3 * RANK :] = block[:, j * RANK : (j + 1) * RANK]


def sum_kernel(parts, out):
    total = parts[0].astype(F32)
    for peer in range(1, parts.shape[0]):
        total = total + parts[peer].astype(F32)
    out[...] = jnp.broadcast_to(total.astype(BF), out.shape)


def final_kernel(parts, down, up):
    rows = up.shape[0]
    down[...] = parts[0, :, : 3 * RANK].astype(F32)
    for j in range(up.shape[1] // RANK):
        up[:, j * RANK : (j + 1) * RANK] = parts[0, j * rows : (j + 1) * rows, 3 * RANK :].astype(
            F32
        )


def whole(shape):
    return pl.BlockSpec(shape, lambda *_: (0,) * len(shape))


def body(
    queries,
    tree_keys,
    tree_values,
    cache_keys,
    cache_values,
    parents,
    cache_lengths,
    accepted_counts,
    dest_map,
    low_hidden,
    mid_hidden,
    norm_gains,
    merge_down,
    merge_up,
    out_grad,
):
    count, width = low_hidden.shape
    branches = parents.shape[0]
    slots = out_grad.shape[0]
    ny, nzx, nh = lax.axis_size("y"), lax.axis_size("zx"), lax.axis_size("head")
    peers = ny * nzx
    smem = pl.BlockSpec(memory_space=pltpu.SMEM)
    row_block = pl.BlockSpec((TREE, width), lambda b: (b, 0))
    cache_block = pl.BlockSpec((1, CACHE, HEAD_DIM), lambda b: (b, 0, 0))

    received = lax.all_to_all(
        out_grad.reshape(peers, slots // peers, width), ("y", "zx"), 0, 0, tiled=True
    ).reshape(slots, width)
    turned, partial = pl.pallas_call(
        feature_kernel,
        grid=(branches,),
        in_specs=[
            smem,
            smem,
            whole((branches, TREE)),
            row_block,
            whole((count, HEAD_DIM)),
            whole((count, HEAD_DIM)),
            cache_block,
            cache_block,
            row_block,
            row_block,
            whole((3, width)),
            whole((width, 3 * RANK)),
        ],
        out_specs=[whole((3, width, count)), whole((count, 4 * RANK))],
        out_shape=[
            jax.ShapeDtypeStruct((3, width, count), BF),
            jax.ShapeDtypeStruct((count, 4 * RANK), BF),
        ],
        scratch_shapes=[
            pltpu.VMEM((count, count), F32),
            pltpu.VMEM((3, count, width), BF),
            pltpu.VMEM((count, RANK), BF),
        ],
        compiler_params=params(),
        cost_estimate=pl.CostEstimate(
            flops=400_000_000, bytes_accessed=8_000_000, transcendentals=600_000
        ),
        name="features",
    )(
        cache_lengths,
        accepted_counts,
        parents,
        queries,
        tree_keys,
        tree_values,
        cache_keys,
        cache_values,
        low_hidden,
        mid_hidden,
        norm_gains,
        merge_down,
    )
    sent, chosen = pl.pallas_call(
        back_kernel,
        out_shape=[
            jax.ShapeDtypeStruct((count, 5 * RANK), BF),
            jax.ShapeDtypeStruct((count, slots), BF),
        ],
        compiler_params=params(),
        name="back",
    )(dest_map, received, merge_up, partial)
    share = count // nh
    parts = lax.all_to_all(sent.reshape(nh, share, 5 * RANK), "head", 0, 0, tiled=True)
    merged = pl.pallas_call(
        merge_kernel,
        out_shape=jax.ShapeDtypeStruct((nh, share, 4 * RANK), BF),
        compiler_params=params(),
        name="merge",
    )(parts)
    merged = lax.all_to_all(merged, "head", 0, 0, tiled=True).reshape(count, 4 * RANK)
    block = width // nzx
    grads = pl.pallas_call(
        grads_kernel,
        grid=(nzx,),
        in_specs=[
            pl.BlockSpec((3, block, count), lambda i: (0, i, 0)),
            whole((slots, width)),
            whole((count, 4 * RANK)),
            whole((count, slots)),
        ],
        out_specs=pl.BlockSpec((1, block, 4 * RANK), lambda i: (i, 0, 0)),
        out_shape=jax.ShapeDtypeStruct((nzx, block, 4 * RANK), BF),
        scratch_shapes=[pltpu.VMEM((RANK, width), BF)],
        compiler_params=params(),
        name="grads",
    )(turned, received, merged, chosen)
    grads = lax.all_to_all(grads, "zx", 0, 0, tiled=True)
    piece = block // ny
    grads = pl.pallas_call(
        sum_kernel,
        grid=(ny,),
        in_specs=[pl.BlockSpec((nzx, piece, 4 * RANK), lambda i: (0, i, 0))],
        out_specs=pl.BlockSpec((1, piece, 4 * RANK), lambda i: (i, 0, 0)),
        out_shape=jax.ShapeDtypeStruct((ny, piece, 4 * RANK), BF),
        compiler_params=params(),
        name="sum_zx",
    )(grads)
    grads = lax.all_to_all(grads, "y", 0, 0, tiled=True)
    grads = pl.pallas_call(
        sum_kernel,
        out_shape=jax.ShapeDtypeStruct((ny, piece, 4 * RANK), BF),
        compiler_params=params(),
        name="sum_y",
    )(grads)
    grads = lax.all_to_all(grads, "y", 0, 0, tiled=True).reshape(block, 4 * RANK)
    grads = lax.all_to_all(
        jnp.broadcast_to(grads[None], (nzx, block, 4 * RANK)), "zx", 0, 0, tiled=True
    )
    return pl.pallas_call(
        final_kernel,
        grid=(nzx,),
        in_specs=[pl.BlockSpec((1, block, 4 * RANK), lambda i: (i, 0, 0))],
        out_specs=[
            pl.BlockSpec((block, 3 * RANK), lambda i: (i, 0)),
            pl.BlockSpec((RANK // nzx, width), lambda i: (i, 0)),
        ],
        out_shape=[
            jax.ShapeDtypeStruct((width, 3 * RANK), F32),
            jax.ShapeDtypeStruct((RANK, width), F32),
        ],
        compiler_params=params(),
        name="final",
    )(grads)


def solution(mesh):
    fine = Mesh(mesh.devices.reshape(8, 8, 8), ("y", "zx", "head"))
    dp = ("y", "zx")
    placed = (
        P(dp, "head"),
        P(dp, "head"),
        P(dp, "head"),
        P(dp, None, "head"),
        P(dp, None, "head"),
        P(dp, None),
        P(dp),
        P(dp),
        P(dp, None),
        P(dp, "head"),
        P(dp, "head"),
        P(None, "head"),
        P("head", None),
        P(None, "head"),
        P(dp, "head"),
    )
    return jax.shard_map(
        body,
        mesh=fine,
        in_specs=placed,
        out_specs=(P("head", None), P(None, "head")),
        check_vma=False,
    )
```

```python
import jax
import jax.numpy as jnp
from jax import lax
from jax.experimental import pallas as pl
from jax.experimental.pallas import tpu as pltpu
from jax.sharding import Mesh, PartitionSpec as P

MODEL_WIDTH = 16384
HEAD_DIM = 128
TREE = 16
CACHE = 128
RANK = 128
MOST = 3
NX = 4
EPSILON = 1e-05
MASKED = -1e30
BF = jnp.bfloat16
F32 = jnp.float32
VMEM_LIMIT = 48 * 1024 * 1024


def params():
    return pltpu.CompilerParams(vmem_limit_bytes=VMEM_LIMIT)


def iota(shape, dim):
    return lax.broadcasted_iota(jnp.int32, shape, dim)


def dot(a, b):
    return jnp.dot(a, b, preferred_element_type=F32)


def dot_nt(a, b):
    return lax.dot_general(a, b, (((1,), (1,)), ((), ())), preferred_element_type=F32)


def dot_tn(a, b):
    return lax.dot_general(a, b, (((0,), (0,)), ((), ())), preferred_element_type=F32)


def feature_kernel(
    place,
    lengths,
    counts,
    parents,
    queries,
    tree_keys,
    tree_values,
    cache_keys,
    cache_values,
    low,
    mid,
    gains,
    merge_down,
    own,
    first,
    second,
    third,
    partial,
    reach,
    rows,
    squares,
):
    branch = pl.program_id(0)
    branches = pl.num_programs(0)
    count, width = rows.shape[1], rows.shape[2]
    heads = width // HEAD_DIM

    @pl.when(branch == 0)
    def _():
        groups = parents.shape[0]
        owner = (iota((count, groups), 0) // TREE == iota((count, groups), 1)).astype(F32)
        spread = jnp.dot(owner, parents[...].astype(F32), preferred_element_type=F32)
        same = iota((count, TREE), 0) % TREE == iota((count, TREE), 1)
        parent = jnp.sum(jnp.where(same, spread, 0.0), axis=1, keepdims=True).astype(jnp.int32)
        row, column = iota((count, count), 0), iota((count, count), 1)
        linked = (column == row) | ((parent >= 0) & (column == row // TREE * TREE + parent))
        reached = jnp.where(linked, 1.0, 0.0)
        for _ in range((TREE - 1).bit_length()):
            step = reached.astype(BF)
            reached = jnp.minimum(dot(step, step), 1.0)
        reach[...] = reached

    start = pl.multiple_of(branch * TREE, TREE)
    here = pl.ds(start, TREE)
    query = queries[...]
    query = jnp.concatenate(
        [query[:, h * HEAD_DIM : (h + 1) * HEAD_DIM] for h in range(heads)], axis=0
    )
    keys = jnp.concatenate([cache_keys[0], tree_keys[...]], axis=0)
    values = jnp.concatenate([cache_values[0], tree_values[...]], axis=0)
    scores = dot_nt(query, keys) * (HEAD_DIM**-0.5)
    live = jnp.where(iota((TREE, CACHE), 1) < lengths[branch], 1.0, 0.0)
    seen = jnp.concatenate([live, reach[here, :]], axis=1) > 0.5
    scores = jnp.where(seen[None], scores.reshape(heads, TREE, CACHE + count), MASKED)
    weights = jnp.exp(scores - jnp.max(scores, axis=2, keepdims=True))
    probs = (weights / jnp.sum(weights, axis=2, keepdims=True)).astype(BF)
    attended = dot(probs.reshape(heads * TREE, CACHE + count), values).astype(BF)
    attended = jnp.concatenate(
        [attended[h * TREE : (h + 1) * TREE, :] for h in range(heads)], axis=1
    )
    kept = iota((TREE, 1), 0) < counts[branch]
    lane = iota((TREE, RANK), 1)
    totals = jnp.zeros((TREE, RANK), F32)
    for layer, feature in enumerate((low[...], mid[...], attended)):
        feature = jnp.where(kept, feature.astype(F32), 0.0)
        total = jnp.sum(feature * feature, axis=1, keepdims=True)
        totals = totals + jnp.where(lane == layer, total, 0.0)
        gain = gains[layer : layer + 1, :].astype(F32)
        rows[layer, here, :] = (feature * gain).astype(BF)
    squares[here, :] = totals

    @pl.when(branch == branches - 1)
    def _():
        block = own.shape[1]
        for layer in range(3):
            columns = slice(layer * RANK, (layer + 1) * RANK)
            partial[:, columns] = dot(rows[layer], merge_down[:, columns])
            for k, out in enumerate((own, first, second, third)):
                chunk = (place[0] + k) % (width // block)
                chunk = pl.ds(pl.multiple_of(chunk * block, block), block)
                out[layer] = rows[layer, :, chunk].T
        partial[:, 3 * RANK :] = squares[...]


def pack_kernel(grads, merge_up, out, rows):
    peers, height = out.shape[0], out.shape[1]
    slots = grads.shape[0] // (peers // NX)
    blocks = grads.shape[1] // NX // RANK
    wide = grads[...].astype(F32)
    products = dot_nt(grads[...], merge_up[...])
    rows[:, blocks * slots :, :] = jnp.zeros((peers, height - blocks * slots, RANK), F32)
    for x in range(NX):
        for b in range(blocks):
            column = (x * blocks + b) * RANK
            for g in range(peers // NX):
                rows[g * NX + x, b * slots : (b + 1) * slots, :] = wide[
                    g * slots : (g + 1) * slots, column : column + RANK
                ]
    for d in range(peers):
        rows[d, blocks * slots : blocks * slots + MOST, :] = products[d * MOST : (d + 1) * MOST, :]
    out[...] = rows[...].astype(BF)


def unpack_kernel(received, out, rows):
    peers = received.shape[0]
    slots = out.shape[0] // peers
    for j in range(peers):
        wide = received[j].astype(F32)
        for b in range(out.shape[1] // RANK):
            rows[j * slots : (j + 1) * slots, b * RANK : (b + 1) * RANK] = wide[
                b * slots : (b + 1) * slots, :
            ]
    out[...] = rows[...].astype(BF)


def pick_kernel(place, targets, received, partial, keep, give, info, rows, notes):
    count = rows.shape[0]
    half = keep.shape[0]
    peers = received.shape[0]
    tail = received[:, received.shape[1] - 8 :, :].astype(F32).reshape(peers * 8, RANK).astype(BF)
    target = targets[...]
    named = (target == iota((count, peers), 1)).astype(F32)
    earlier = (iota((count, count), 0) > iota((count, count), 1)).astype(BF)
    before = dot(earlier, named.astype(BF))
    rank = jnp.sum(before * named, axis=1, keepdims=True)
    chosen = target * 8 + rank.astype(jnp.int32) == iota((count, peers * 8), 1)
    rows[:, : 3 * RANK] = partial[:, : 3 * RANK]
    rows[:, 3 * RANK : 4 * RANK] = dot(chosen.astype(BF), tail)
    rows[:, 4 * RANK :] = partial[:, 3 * RANK :]
    lane = iota((count, RANK), 1)
    notes[...] = jnp.where(lane == 6, target.astype(F32), jnp.where(lane == 7, rank, 0.0))
    mine = pl.ds(pl.multiple_of(place[1] * half, half), half)
    keep[...] = rows[mine, :]
    info[...] = notes[mine, :]
    give[...] = rows[pl.ds(pl.multiple_of((1 - place[1]) * half, half), half), :]


def pair_kernel(keep, got, out):
    total = keep[...] + got[...]
    squares = total[:, 4 * RANK :]
    rough = squares.astype(BF).astype(F32)
    lane = iota(squares.shape, 1)
    for i in range(3):
        rest = squares[:, i : i + 1] - rough[:, i : i + 1]
        rough = jnp.where(lane == 3 + i, rest, rough)
    out[:, : 4 * RANK] = total[:, : 4 * RANK].astype(BF)
    out[:, 4 * RANK :] = rough.astype(BF)


def merge_kernel(parts, info, out):
    total = parts[0].astype(F32)
    for peer in range(1, parts.shape[0]):
        total = total + parts[peer].astype(F32)
    squares = total[:, 4 * RANK :]
    inverse = [
        lax.rsqrt((squares[:, i : i + 1] + squares[:, 3 + i : 4 + i]) / MODEL_WIDTH + EPSILON)
        for i in range(3)
    ]
    mixed = inverse[0] * total[:, :RANK]
    for i in (1, 2):
        mixed = mixed + inverse[i] * total[:, i * RANK : (i + 1) * RANK]
    back = total[:, 3 * RANK : 4 * RANK]
    gate = 1.0 / (1.0 + jnp.exp(-mixed))
    out[:, :RANK] = (back * gate * (1.0 + mixed * (1.0 - gate))).astype(BF)
    out[:, RANK : 2 * RANK] = (mixed * gate).astype(BF)
    notes = info[...]
    lane = iota(notes.shape, 1)
    for i in range(3):
        rough = inverse[i].astype(BF).astype(F32)
        notes = jnp.where(lane == i, rough, notes)
        notes = jnp.where(lane == 3 + i, inverse[i] - rough, notes)
    out[:, 2 * RANK :] = notes.astype(BF)


def grads_kernel(place, own, first, second, third, slots, merged, out):
    blocks = slots.shape[1] // RANK
    peer_slots = NX * MOST
    down = [None] * 3
    placed = None
    for k, turned in enumerate((own, first, second, third)):
        source = (place[0] + NX - k) % NX
        rows = jnp.concatenate([merged[2 * source], merged[2 * source + 1]], axis=0)
        notes = rows[:, 2 * RANK :].astype(F32)
        grad = rows[:, :RANK].astype(F32)
        for i in range(3):
            inverse = notes[:, i : i + 1] + notes[:, 3 + i : 4 + i]
            term = dot(turned[i], (inverse * grad).astype(BF))
            down[i] = term if down[i] is None else down[i] + term
        slot = notes[:, 6:7].astype(jnp.int32) * peer_slots + notes[:, 7:8].astype(jnp.int32)
        slot = slot + source * MOST
        chosen = (slot == iota((rows.shape[0], slots.shape[0]), 1)).astype(BF)
        term = dot_tn(rows[:, RANK : 2 * RANK], chosen)
        placed = term if placed is None else placed + term
    for i in range(3):
        out[:, i * RANK : (i + 1) * RANK] = down[i].astype(BF)
    up = dot(placed.astype(BF), slots[...]).astype(BF)
    for b in range(blocks):
        out[b * RANK : (b + 1) * RANK, 3 * RANK :] = up[:, b * RANK : (b + 1) * RANK]


def sum_kernel(parts, out):
    total = parts[0].astype(F32)
    for peer in range(1, parts.shape[0]):
        total = total + parts[peer].astype(F32)
    out[...] = jnp.broadcast_to(total.astype(BF)[None], out.shape)


def final_kernel(parts, down, up):
    down[...] = parts[0, :, : 3 * RANK].astype(F32)
    for b in range(up.shape[1] // RANK):
        columns = slice(b * RANK, (b + 1) * RANK)
        up[:, columns] = parts[0, columns, 3 * RANK :].astype(F32)


def whole(shape):
    return pl.BlockSpec(shape, lambda *_: (0,) * len(shape))


def shape(dims, kind=BF):
    return jax.ShapeDtypeStruct(dims, kind)


def call(kernel, name, out_shape, *args, scratch=(), flops=1_000_000):
    smem = pl.BlockSpec(memory_space=pltpu.SMEM)
    vmem = pl.BlockSpec(memory_space=pltpu.VMEM)
    return pl.pallas_call(
        kernel,
        in_specs=[smem if a.ndim == 1 else vmem for a in args],
        out_shape=out_shape,
        scratch_shapes=[pltpu.VMEM(*s) for s in scratch],
        compiler_params=params(),
        cost_estimate=pl.CostEstimate(flops=flops, bytes_accessed=2_000_000, transcendentals=0),
        name=name,
    )(*args)


def spread(array, n, axes):
    return lax.all_to_all(jnp.broadcast_to(array[None], (n, *array.shape)), axes, 0, 0, tiled=True)


def body(
    queries,
    tree_keys,
    tree_values,
    cache_keys,
    cache_values,
    parents,
    cache_lengths,
    accepted_counts,
    dest_map,
    low_hidden,
    mid_hidden,
    norm_gains,
    merge_down,
    merge_up,
    out_grad,
):
    count, width = low_hidden.shape
    branches = parents.shape[0]
    ny, nzl, nc = lax.axis_size("y"), lax.axis_size("zl"), lax.axis_size("c")
    nzh = lax.axis_size("zh")
    peers = ny * nzl * NX
    block = width // NX
    place = jnp.stack([lax.axis_index("x"), lax.axis_index("c")]).astype(jnp.int32)
    smem = pl.BlockSpec(memory_space=pltpu.SMEM)
    row_block = pl.BlockSpec((TREE, width), lambda b: (b, 0))
    cache_block = pl.BlockSpec((1, CACHE, HEAD_DIM), lambda b: (b, 0, 0))

    height = block // RANK * NX * MOST + 8
    packed = call(
        pack_kernel,
        "pack",
        shape((peers, height, RANK)),
        out_grad,
        merge_up,
        scratch=[((peers, height, RANK), F32)],
    )
    received = lax.all_to_all(packed, ("y", "zl", "x"), 0, 0, tiled=True)
    *turned, partial = pl.pallas_call(
        feature_kernel,
        grid=(branches,),
        in_specs=[
            smem,
            smem,
            smem,
            whole((branches, TREE)),
            row_block,
            whole((count, HEAD_DIM)),
            whole((count, HEAD_DIM)),
            cache_block,
            cache_block,
            row_block,
            row_block,
            whole((3, width)),
            whole((width, 3 * RANK)),
        ],
        out_specs=[whole((3, block, count))] * NX + [whole((count, 4 * RANK))],
        out_shape=[shape((3, block, count))] * NX + [shape((count, 4 * RANK), F32)],
        scratch_shapes=[
            pltpu.VMEM((count, count), F32),
            pltpu.VMEM((3, count, width), BF),
            pltpu.VMEM((count, RANK), F32),
        ],
        compiler_params=params(),
        cost_estimate=pl.CostEstimate(
            flops=400_000_000, bytes_accessed=8_000_000, transcendentals=600_000
        ),
        name="features",
    )(
        place,
        cache_lengths,
        accepted_counts,
        parents,
        queries,
        tree_keys,
        tree_values,
        cache_keys,
        cache_values,
        low_hidden,
        mid_hidden,
        norm_gains,
        merge_down,
    )
    for k in range(1, NX):
        turned[k] = lax.ppermute(turned[k], "x", [(i, (i + k) % NX) for i in range(NX)])
    half = count // nc
    keep, give, info = call(
        pick_kernel,
        "pick",
        [shape((half, 5 * RANK), F32), shape((half, 5 * RANK), F32), shape((half, RANK), F32)],
        place,
        dest_map,
        received,
        partial,
        scratch=[((count, 5 * RANK), F32), ((count, RANK), F32)],
    )
    got = lax.ppermute(give, "c", [(i, 1 - i) for i in range(nc)])
    paired = call(pair_kernel, "pair", shape((half, 5 * RANK)), keep, got)
    parts = spread(paired, nzh, "zh")
    merged = call(merge_kernel, "merge", shape((half, 3 * RANK)), parts, info)
    merged = spread(merged, NX * nc, ("x", "c"))
    slots = call(
        unpack_kernel,
        "unpack",
        shape((peers * NX * MOST, block)),
        received,
        scratch=[((peers * NX * MOST, block), F32)],
    )
    grads = call(
        grads_kernel, "grads", shape((block, 4 * RANK)), place, *turned, slots, merged
    )
    piece = block // (nzl * ny)
    grads = lax.all_to_all(
        grads.reshape(nzl * ny, piece, 4 * RANK), ("zl", "y"), 0, 0, tiled=True
    )
    grads = call(sum_kernel, "total", shape((ny, piece, 4 * RANK)), grads)
    grads = lax.all_to_all(grads, "y", 0, 0, tiled=True).reshape(ny * piece, 4 * RANK)
    grads = spread(grads, nzl * NX, ("zl", "x"))
    rows = ny * piece
    return pl.pallas_call(
        final_kernel,
        grid=(nzl * NX,),
        in_specs=[pl.BlockSpec((1, rows, 4 * RANK), lambda i: (i % nzl * NX + i // nzl, 0, 0))],
        out_specs=[
            pl.BlockSpec((rows, 3 * RANK), lambda i: (i, 0)),
            pl.BlockSpec((RANK, rows), lambda i: (0, i)),
        ],
        out_shape=[shape((width, 3 * RANK), F32), shape((RANK, width), F32)],
        compiler_params=params(),
        name="final",
    )(grads)


def solution(mesh):
    fine = Mesh(mesh.devices.reshape(8, 2, NX, 4, 2), ("y", "zl", "x", "zh", "c"))
    dp, head = ("y", "zl", "x"), ("zh", "c")
    placed = (
        P(dp, head),
        P(dp, head),
        P(dp, head),
        P(dp, None, head),
        P(dp, None, head),
        P(dp, None),
        P(dp),
        P(dp),
        P(dp, None),
        P(dp, head),
        P(dp, head),
        P(None, head),
        P(head, None),
        P(None, head),
        P(dp, head),
    )
    return jax.shard_map(
        body,
        mesh=fine,
        in_specs=placed,
        out_specs=(P(head, None), P(None, head)),
        check_vma=False,
    )
```

```python
import jax
import jax.numpy as jnp
from jax import lax
from jax.experimental import pallas as pl
from jax.experimental.pallas import tpu as pltpu
from jax.sharding import Mesh, PartitionSpec as P

MODEL_WIDTH = 16384
HEAD_DIM = 128
TREE = 16
CACHE = 128
RANK = 128
MOST = 3
NX = 4
PEERS = 64
EPSILON = 1e-05
MASKED = -1e30
BF = jnp.bfloat16
F32 = jnp.float32
MIB = 1024 * 1024


def params(limit=32):
    return pltpu.CompilerParams(vmem_limit_bytes=limit * MIB)


def iota(shape, dim):
    return lax.broadcasted_iota(jnp.int32, shape, dim)


def dot(a, b):
    return jnp.dot(a, b, preferred_element_type=F32)


def dot_nt(a, b):
    return lax.dot_general(a, b, (((1,), (1,)), ((), ())), preferred_element_type=F32)


def dot_tn(a, b):
    return lax.dot_general(a, b, (((0,), (0,)), ((), ())), preferred_element_type=F32)


def feature_kernel(
    place,
    lengths,
    counts,
    targets,
    parents,
    queries,
    tree_keys,
    tree_values,
    cache_keys,
    cache_values,
    low,
    mid,
    gains,
    merge_down,
    own,
    first,
    second,
    third,
    partial,
    reach,
    rows,
    squares,
):
    branch = pl.program_id(0)
    branches = pl.num_programs(0)
    count, width = rows.shape[1], rows.shape[2]
    heads = width // HEAD_DIM

    @pl.when(branch == 0)
    def _():
        groups = parents.shape[0]
        owner = (iota((count, groups), 0) // TREE == iota((count, groups), 1)).astype(F32)
        spread = jnp.dot(owner, parents[...].astype(F32), preferred_element_type=F32)
        same = iota((count, TREE), 0) % TREE == iota((count, TREE), 1)
        parent = jnp.sum(jnp.where(same, spread, 0.0), axis=1, keepdims=True).astype(jnp.int32)
        row, column = iota((count, count), 0), iota((count, count), 1)
        linked = (column == row) | ((parent >= 0) & (column == row // TREE * TREE + parent))
        reached = jnp.where(linked, 1.0, 0.0)
        for _ in range((TREE - 1).bit_length()):
            step = reached.astype(BF)
            reached = jnp.minimum(dot(step, step), 1.0)
        reach[...] = reached

    start = pl.multiple_of(branch * TREE, TREE)
    here = pl.ds(start, TREE)
    query = queries[...]
    query = jnp.concatenate(
        [query[:, h * HEAD_DIM : (h + 1) * HEAD_DIM] for h in range(heads)], axis=0
    )
    keys = jnp.concatenate([cache_keys[0], tree_keys[...]], axis=0)
    values = jnp.concatenate([cache_values[0], tree_values[...]], axis=0)
    scores = dot_nt(query, keys) * (HEAD_DIM**-0.5)
    live = jnp.where(iota((TREE, CACHE), 1) < lengths[branch], 1.0, 0.0)
    seen = jnp.concatenate([live, reach[here, :]], axis=1) > 0.5
    scores = jnp.where(seen[None], scores.reshape(heads, TREE, CACHE + count), MASKED)
    weights = jnp.exp(scores - jnp.max(scores, axis=2, keepdims=True))
    probs = (weights / jnp.sum(weights, axis=2, keepdims=True)).astype(BF)
    attended = dot(probs.reshape(heads * TREE, CACHE + count), values).astype(BF)
    attended = jnp.concatenate(
        [attended[h * TREE : (h + 1) * TREE, :] for h in range(heads)], axis=1
    )
    kept = iota((TREE, 1), 0) < counts[branch]
    lane = iota((TREE, RANK), 1)
    totals = jnp.zeros((TREE, RANK), F32)
    for layer, feature in enumerate((low[...], mid[...], attended)):
        feature = jnp.where(kept, feature.astype(F32), 0.0)
        total = jnp.sum(feature * feature, axis=1, keepdims=True)
        totals = totals + jnp.where(lane == layer, total, 0.0)
        gain = gains[layer : layer + 1, :].astype(F32)
        rows[layer, here, :] = (feature * gain).astype(BF)
    squares[here, :] = totals

    @pl.when(branch == branches - 1)
    def _():
        block = own.shape[1]
        for layer in range(3):
            columns = slice(layer * RANK, (layer + 1) * RANK)
            partial[:, columns] = dot(rows[layer], merge_down[:, columns])
            for k, out in enumerate((own, first, second, third)):
                chunk = (place[0] + k) % (width // block)
                chunk = pl.ds(pl.multiple_of(chunk * block, block), block)
                out[layer] = rows[layer, :, chunk].T
        target = targets[...]
        named = (target == iota((count, PEERS), 1)).astype(F32)
        earlier = (iota((count, count), 0) > iota((count, count), 1)).astype(BF)
        rank = jnp.sum(dot(earlier, named.astype(BF)) * named, axis=1, keepdims=True)
        notes = squares[...]
        lane = iota((count, RANK), 1)
        for i, note in ((6, target.astype(F32)), (7, rank), (8, place[1].astype(F32))):
            notes = jnp.where(lane == i, note, notes)
        partial[:, 3 * RANK :] = notes


def pack_kernel(grads, merge_up, out, rows):
    peers, height = out.shape[0], out.shape[1]
    slots = grads.shape[0] // (peers // NX)
    blocks = grads.shape[1] // NX // RANK
    wide = grads[...].astype(F32)
    products = dot_nt(grads[...], merge_up[...])
    rows[:, blocks * slots :, :] = jnp.zeros((peers, height - blocks * slots, RANK), F32)
    for x in range(NX):
        for b in range(blocks):
            column = (x * blocks + b) * RANK
            for g in range(peers // NX):
                rows[g * NX + x, b * slots : (b + 1) * slots, :] = wide[
                    g * slots : (g + 1) * slots, column : column + RANK
                ]
    for d in range(peers):
        rows[d, blocks * slots : blocks * slots + MOST, :] = products[d * MOST : (d + 1) * MOST, :]
    out[...] = rows[...].astype(BF)


def unpack_kernel(received, out, rows):
    peers = received.shape[0]
    slots = out.shape[0] // peers
    for j in range(peers):
        wide = received[j].astype(F32)
        for b in range(out.shape[1] // RANK):
            rows[j * slots : (j + 1) * slots, b * RANK : (b + 1) * RANK] = wide[
                b * slots : (b + 1) * slots, :
            ]
    out[...] = rows[...].astype(BF)


def pick_kernel(received, partial, keep, give, info):
    count = partial.shape[0]
    half = keep.shape[0]
    peers = received.shape[0]
    tail = received[:, received.shape[1] - 8 :, :].astype(F32).reshape(peers * 8, RANK).astype(BF)
    notes = partial[:, 3 * RANK :]
    place = (notes[:, 6:7] * 8.0 + notes[:, 7:8]).astype(jnp.int32)
    chosen = place == iota((count, peers * 8), 1)
    back = dot(chosen.astype(BF), tail)
    upper = notes[:half, 8:9] > 0.5
    for source, start in ((partial[:, : 3 * RANK], 0), (back, 3 * RANK), (notes, 4 * RANK)):
        columns = slice(start, start + source.shape[1])
        keep[:, columns] = jnp.where(upper, source[half:], source[:half])
        give[:, columns] = jnp.where(upper, source[:half], source[half:])
    info[...] = jnp.where(upper, notes[half:], notes[:half])


def pair_kernel(keep, got, first, second, third, out):
    total = keep[...] + got[...]
    squares = total[:, 4 * RANK :]
    rough = squares.astype(BF).astype(F32)
    lane = iota(squares.shape, 1)
    for i in range(3):
        rest = squares[:, i : i + 1] - rough[:, i : i + 1]
        rough = jnp.where(lane == 3 + i, rest, rough)
    rough = jnp.where(lane < 6, rough, 0.0)
    for peer in range(out.shape[0]):
        out[peer, :, : 4 * RANK] = total[:, : 4 * RANK].astype(BF)
        out[peer, :, 4 * RANK :] = rough.astype(BF)


def merge_kernel(parts, info, out):
    total = parts[0].astype(F32)
    for peer in range(1, parts.shape[0]):
        total = total + parts[peer].astype(F32)
    squares = total[:, 4 * RANK :]
    inverse = [
        lax.rsqrt((squares[:, i : i + 1] + squares[:, 3 + i : 4 + i]) / MODEL_WIDTH + EPSILON)
        for i in range(3)
    ]
    mixed = inverse[0] * total[:, :RANK]
    for i in (1, 2):
        mixed = mixed + inverse[i] * total[:, i * RANK : (i + 1) * RANK]
    back = total[:, 3 * RANK : 4 * RANK]
    gate = 1.0 / (1.0 + jnp.exp(-mixed))
    grad = (back * gate * (1.0 + mixed * (1.0 - gate))).astype(BF)
    active = (mixed * gate).astype(BF)
    notes = info[...]
    lane = iota(notes.shape, 1)
    for i in range(3):
        rough = inverse[i].astype(BF).astype(F32)
        notes = jnp.where(lane == i, rough, notes)
        notes = jnp.where(lane == 3 + i, inverse[i] - rough, notes)
    notes = notes.astype(BF)
    for peer in range(out.shape[0]):
        out[peer, :, :RANK] = grad
        out[peer, :, RANK : 2 * RANK] = active
        out[peer, :, 2 * RANK :] = notes


def grads_kernel(place, own, first, second, third, slots, merged, out):
    blocks = slots.shape[1] // RANK
    peer_slots = NX * MOST
    down = [None] * 3
    placed = None
    for k, turned in enumerate((own, first, second, third)):
        source = (place[0] + NX - k) % NX
        rows = jnp.concatenate([merged[2 * source], merged[2 * source + 1]], axis=0)
        notes = rows[:, 2 * RANK :].astype(F32)
        grad = rows[:, :RANK].astype(F32)
        for i in range(3):
            inverse = notes[:, i : i + 1] + notes[:, 3 + i : 4 + i]
            term = dot(turned[i], (inverse * grad).astype(BF))
            down[i] = term if down[i] is None else down[i] + term
        slot = notes[:, 6:7].astype(jnp.int32) * peer_slots + notes[:, 7:8].astype(jnp.int32)
        slot = slot + source * MOST
        chosen = (slot == iota((rows.shape[0], slots.shape[0]), 1)).astype(BF)
        term = dot_tn(rows[:, RANK : 2 * RANK], chosen)
        placed = term if placed is None else placed + term
    for i in range(3):
        out[:, i * RANK : (i + 1) * RANK] = down[i].astype(BF)
    up = dot(placed.astype(BF), slots[...]).astype(BF)
    for b in range(blocks):
        out[b * RANK : (b + 1) * RANK, 3 * RANK :] = up[:, b * RANK : (b + 1) * RANK]


def sum_kernel(parts, out):
    total = parts[0].astype(F32)
    for peer in range(1, parts.shape[0]):
        total = total + parts[peer].astype(F32)
    out[...] = jnp.broadcast_to(total.astype(BF)[None], out.shape)


def final_kernel(parts, down, up):
    down[...] = parts[0, :, : 3 * RANK].astype(F32)
    for b in range(up.shape[1] // RANK):
        columns = slice(b * RANK, (b + 1) * RANK)
        up[:, columns] = parts[0, columns, 3 * RANK :].astype(F32)


def whole(shape):
    return pl.BlockSpec(shape, lambda *_: (0,) * len(shape))


def shape(dims, kind=BF):
    return jax.ShapeDtypeStruct(dims, kind)


def call(kernel, name, out_shape, *args, unread=(), scratch=(), grid=(), limit=32):
    smem = pl.BlockSpec(memory_space=pltpu.SMEM)
    specs = [smem if a.ndim == 1 else whole(a.shape) for a in args]
    specs = specs + [pl.BlockSpec(memory_space=pl.ANY) for _ in unread]
    outs = out_shape if isinstance(out_shape, list) else [out_shape]
    outs = [whole(o.shape) for o in outs]
    return pl.pallas_call(
        kernel,
        grid=grid,
        in_specs=specs,
        out_specs=outs if isinstance(out_shape, list) else outs[0],
        out_shape=out_shape,
        scratch_shapes=[pltpu.VMEM(*s) for s in scratch],
        compiler_params=params(limit),
        cost_estimate=pl.CostEstimate(
            flops=1_000_000, bytes_accessed=2_000_000, transcendentals=0
        ),
        name=name,
    )(*args, *unread)


def body(
    queries,
    tree_keys,
    tree_values,
    cache_keys,
    cache_values,
    parents,
    cache_lengths,
    accepted_counts,
    dest_map,
    low_hidden,
    mid_hidden,
    norm_gains,
    merge_down,
    merge_up,
    out_grad,
):
    count, width = low_hidden.shape
    branches = parents.shape[0]
    nyh, nyl, nzl = lax.axis_size("yh"), lax.axis_size("yl"), lax.axis_size("zl")
    nzh, nc = lax.axis_size("zh"), lax.axis_size("c")
    peers = nyh * nyl * nzl * NX
    block = width // NX
    place = jnp.stack([lax.axis_index("x"), lax.axis_index("c")]).astype(jnp.int32)
    smem = pl.BlockSpec(memory_space=pltpu.SMEM)
    row_block = pl.BlockSpec((TREE, width), lambda b: (b, 0))
    cache_block = pl.BlockSpec((1, CACHE, HEAD_DIM), lambda b: (b, 0, 0))

    height = block // RANK * NX * MOST + 8
    packed = call(
        pack_kernel,
        "pack",
        shape((peers, height, RANK)),
        out_grad,
        merge_up,
        scratch=[((peers, height, RANK), F32)],
        grid=(1,),
        limit=60,
    )
    received = lax.all_to_all(packed, ("yh", "yl", "zl", "x"), 0, 0, tiled=True)
    *turned, partial = pl.pallas_call(
        feature_kernel,
        grid=(branches,),
        in_specs=[
            smem,
            smem,
            smem,
            whole((count, 1)),
            whole((branches, TREE)),
            row_block,
            whole((count, HEAD_DIM)),
            whole((count, HEAD_DIM)),
            cache_block,
            cache_block,
            row_block,
            row_block,
            whole((3, width)),
            whole((width, 3 * RANK)),
        ],
        out_specs=[whole((3, block, count))] * NX + [whole((count, 4 * RANK))],
        out_shape=[shape((3, block, count))] * NX + [shape((count, 4 * RANK), F32)],
        scratch_shapes=[
            pltpu.VMEM((count, count), F32),
            pltpu.VMEM((3, count, width), BF),
            pltpu.VMEM((count, RANK), F32),
        ],
        compiler_params=params(60),
        cost_estimate=pl.CostEstimate(
            flops=400_000_000, bytes_accessed=8_000_000, transcendentals=600_000
        ),
        name="features",
    )(
        place,
        cache_lengths,
        accepted_counts,
        dest_map,
        parents,
        queries,
        tree_keys,
        tree_values,
        cache_keys,
        cache_values,
        low_hidden,
        mid_hidden,
        norm_gains,
        merge_down,
    )
    for k in range(1, NX):
        turned[k] = lax.ppermute(turned[k], "x", [(i, (i + k) % NX) for i in range(NX)])
    half = count // nc
    keep, give, info = call(
        pick_kernel,
        "pick",
        [shape((half, 5 * RANK), F32), shape((half, 5 * RANK), F32), shape((half, RANK), F32)],
        received,
        partial,
    )
    got = lax.ppermute(give, "c", [(i, 1 - i) for i in range(nc)])
    parts = call(
        pair_kernel, "pair", shape((nzh, half, 5 * RANK)), keep, got, unread=turned[1:]
    )
    parts = lax.all_to_all(parts, "zh", 0, 0, tiled=True)
    merged = call(merge_kernel, "merge", shape((NX * nc, half, 3 * RANK)), parts, info)
    merged = lax.all_to_all(merged, ("x", "c"), 0, 0, tiled=True)
    slots = call(
        unpack_kernel,
        "unpack",
        shape((peers * NX * MOST, block)),
        received,
        scratch=[((peers * NX * MOST, block), F32)],
    )
    grads = call(
        grads_kernel, "grads", shape((block, 4 * RANK)), place, *turned, slots, merged
    )
    piece = block // (nzl * nyl * nyh)
    grads = lax.all_to_all(
        grads.reshape(nzl * nyl * nyh, piece, 4 * RANK), ("zl", "yl", "yh"), 0, 0, tiled=True
    )
    grads = call(sum_kernel, "total", shape((nyh, piece, 4 * RANK)), grads)
    rows = nyh * piece
    grads = lax.all_to_all(grads, "yh", 0, 0, tiled=True).reshape(rows, 4 * RANK)
    near = nzl * nyl
    grads = jnp.broadcast_to(grads[None], (near * NX, rows, 4 * RANK))
    grads = lax.all_to_all(grads, ("zl", "yl", "x"), 0, 0, tiled=True)
    return pl.pallas_call(
        final_kernel,
        grid=(near * NX,),
        in_specs=[pl.BlockSpec((1, rows, 4 * RANK), lambda i: (i % near * NX + i // near, 0, 0))],
        out_specs=[
            pl.BlockSpec((rows, 3 * RANK), lambda i: (i, 0)),
            pl.BlockSpec((RANK, rows), lambda i: (0, i)),
        ],
        out_shape=[shape((width, 3 * RANK), F32), shape((RANK, width), F32)],
        compiler_params=params(),
        name="final",
    )(grads)


def solution(mesh):
    fine = Mesh(mesh.devices.reshape(4, 2, 2, NX, 4, 2), ("yh", "yl", "zl", "x", "zh", "c"))
    dp, head = ("yh", "yl", "zl", "x"), ("zh", "c")
    placed = (
        P(dp, head),
        P(dp, head),
        P(dp, head),
        P(dp, None, head),
        P(dp, None, head),
        P(dp, None),
        P(dp),
        P(dp),
        P(dp, None),
        P(dp, head),
        P(dp, head),
        P(None, head),
        P(head, None),
        P(None, head),
        P(dp, head),
    )
    return jax.shard_map(
        body,
        mesh=fine,
        in_specs=placed,
        out_specs=(P(head, None), P(None, head)),
        check_vma=False,
    )
```

```python
import jax
import jax.numpy as jnp
from jax import lax
from jax.experimental import pallas as pl
from jax.experimental.pallas import tpu as pltpu
from jax.sharding import Mesh, PartitionSpec as P

MODEL_WIDTH = 16384
HEAD_DIM = 128
TREE = 16
CACHE = 128
RANK = 128
MOST = 3
NX = 4
PEERS = 64
EPSILON = 1e-05
MASKED = -1e30
BF = jnp.bfloat16
F32 = jnp.float32
MIB = 1024 * 1024


def params(limit=32):
    return pltpu.CompilerParams(vmem_limit_bytes=limit * MIB)


def iota(shape, dim):
    return lax.broadcasted_iota(jnp.int32, shape, dim)


def dot(a, b):
    return jnp.dot(a, b, preferred_element_type=F32)


def dot_nt(a, b):
    return lax.dot_general(a, b, (((1,), (1,)), ((), ())), preferred_element_type=F32)


def dot_tn(a, b):
    return lax.dot_general(a, b, (((0,), (0,)), ((), ())), preferred_element_type=F32)


def feature_kernel(
    place,
    lengths,
    counts,
    targets,
    parents,
    queries,
    tree_keys,
    tree_values,
    cache_keys,
    cache_values,
    low,
    mid,
    gains,
    merge_down,
    own,
    first,
    second,
    third,
    partial,
    reach,
    rows,
    squares,
    turned,
    sent,
):
    together = cache_keys.shape[0]
    count, width = rows.shape[1], rows.shape[2]
    heads = width // HEAD_DIM

    @pl.when(pl.program_id(0) == 0)
    def _():
        groups = parents.shape[0]
        owner = (iota((count, groups), 0) // TREE == iota((count, groups), 1)).astype(F32)
        spread = jnp.dot(owner, parents[...].astype(F32), preferred_element_type=F32)
        same = iota((count, TREE), 0) % TREE == iota((count, TREE), 1)
        parent = jnp.sum(jnp.where(same, spread, 0.0), axis=1, keepdims=True).astype(jnp.int32)
        row, column = iota((count, count), 0), iota((count, count), 1)
        linked = (column == row) | ((parent >= 0) & (column == row // TREE * TREE + parent))
        reached = jnp.where(linked, 1.0, 0.0)
        for _ in range((TREE - 1).bit_length()):
            step = reached.astype(BF)
            reached = jnp.minimum(dot(step, step), 1.0)
        reach[...] = reached

    for j in range(together):
        branch = pl.program_id(0) * together + j
        start = pl.multiple_of(branch * TREE, TREE)
        mine = slice(j * TREE, (j + 1) * TREE)
        here = pl.ds(start, TREE)
        query = queries[mine, :]
        query = jnp.concatenate(
            [query[:, h * HEAD_DIM : (h + 1) * HEAD_DIM] for h in range(heads)], axis=0
        )
        keys = jnp.concatenate([cache_keys[j], tree_keys[...]], axis=0)
        values = jnp.concatenate([cache_values[j], tree_values[...]], axis=0)
        scores = dot_nt(query, keys) * (HEAD_DIM**-0.5)
        live = jnp.where(iota((TREE, CACHE), 1) < lengths[branch], 1.0, 0.0)
        seen = jnp.concatenate([live, reach[here, :]], axis=1) > 0.5
        scores = jnp.where(seen[None], scores.reshape(heads, TREE, CACHE + count), MASKED)
        weights = jnp.exp(scores - jnp.max(scores, axis=2, keepdims=True))
        probs = (weights / jnp.sum(weights, axis=2, keepdims=True)).astype(BF)
        attended = dot(probs.reshape(heads * TREE, CACHE + count), values).astype(BF)
        attended = jnp.concatenate(
            [attended[h * TREE : (h + 1) * TREE, :] for h in range(heads)], axis=1
        )
        kept = iota((TREE, 1), 0) < counts[branch]
        lane = iota((TREE, RANK), 1)
        totals = jnp.zeros((TREE, RANK), F32)
        for layer, feature in enumerate((low[mine, :], mid[mine, :], attended)):
            feature = jnp.where(kept, feature.astype(F32), 0.0)
            total = jnp.sum(feature * feature, axis=1, keepdims=True)
            totals = totals + jnp.where(lane == layer, total, 0.0)
            gain = gains[layer : layer + 1, :].astype(F32)
            rows[layer, here, :] = (feature * gain).astype(BF)
        squares[here, :] = totals

    @pl.when(pl.program_id(0) == pl.num_programs(0) - 1)
    def _():
        block = own.shape[1]
        copies = []
        for k, out in enumerate((own, first, second, third)):
            chunk = (place[0] + k) % (width // block)
            chunk = pl.ds(pl.multiple_of(chunk * block, block), block)
            for layer in range(3):
                turned[k, layer] = rows[layer, :, chunk].T
            copies.append(pltpu.make_async_copy(turned.at[k], out, sent.at[k]))
            copies[k].start()
        for layer in range(3):
            columns = slice(layer * RANK, (layer + 1) * RANK)
            partial[:, columns] = dot(rows[layer], merge_down[:, columns])
        target = targets[...]
        named = (target == iota((count, PEERS), 1)).astype(F32)
        earlier = (iota((count, count), 0) > iota((count, count), 1)).astype(BF)
        rank = jnp.sum(dot(earlier, named.astype(BF)) * named, axis=1, keepdims=True)
        notes = squares[...]
        lane = iota((count, RANK), 1)
        for i, note in ((6, target.astype(F32)), (7, rank), (8, place[1].astype(F32))):
            notes = jnp.where(lane == i, note, notes)
        partial[:, 3 * RANK :] = notes
        for copy in copies:
            copy.wait()


def products_kernel(grads, merge_up, out, rows):
    products = dot_nt(grads[...], merge_up[...])
    rows[...] = jnp.zeros_like(rows)
    for d in range(out.shape[0]):
        rows[d, :MOST, :] = products[d * MOST : (d + 1) * MOST, :]
    out[...] = rows[...].astype(BF)


def pack_kernel(grads, after, out, rows):
    peers = out.shape[0]
    slots = grads.shape[0] // (peers // NX)
    blocks = grads.shape[1] // NX // RANK
    wide = grads[...].astype(F32)
    for x in range(NX):
        for b in range(blocks):
            column = (x * blocks + b) * RANK
            for g in range(peers // NX):
                rows[g * NX + x, b * slots : (b + 1) * slots, :] = wide[
                    g * slots : (g + 1) * slots, column : column + RANK
                ]
    out[...] = rows[...].astype(BF)


def unpack_kernel(received, out, rows):
    peers = received.shape[0]
    slots = out.shape[0] // peers
    for j in range(peers):
        wide = received[j].astype(F32)
        for b in range(out.shape[1] // RANK):
            rows[j * slots : (j + 1) * slots, b * RANK : (b + 1) * RANK] = wide[
                b * slots : (b + 1) * slots, :
            ]
    out[...] = rows[...].astype(BF)


def pick_kernel(received, partial, keep, give, info):
    count = partial.shape[0]
    half = keep.shape[0]
    peers = received.shape[0]
    tail = received[...].astype(F32).reshape(peers * 8, RANK).astype(BF)
    notes = partial[:, 3 * RANK :]
    place = (notes[:, 6:7] * 8.0 + notes[:, 7:8]).astype(jnp.int32)
    chosen = place == iota((count, peers * 8), 1)
    back = dot(chosen.astype(BF), tail)
    upper = notes[:half, 8:9] > 0.5
    for source, start in ((partial[:, : 3 * RANK], 0), (back, 3 * RANK), (notes, 4 * RANK)):
        columns = slice(start, start + source.shape[1])
        keep[:, columns] = jnp.where(upper, source[half:], source[:half])
        give[:, columns] = jnp.where(upper, source[:half], source[half:])
    info[...] = jnp.where(upper, notes[half:], notes[:half])


def pair_kernel(keep, got, first, out):
    total = keep[...] + got[...]
    squares = total[:, 4 * RANK :]
    rough = squares.astype(BF).astype(F32)
    lane = iota(squares.shape, 1)
    for i in range(3):
        rest = squares[:, i : i + 1] - rough[:, i : i + 1]
        rough = jnp.where(lane == 3 + i, rest, rough)
    rough = jnp.where(lane < 6, rough, 0.0)
    out[:, : 4 * RANK] = total[:, : 4 * RANK].astype(BF)
    out[:, 4 * RANK :] = rough.astype(BF)


def merge_kernel(own, near, far, last, info, second, third, out):
    total = own[...].astype(F32)
    for part in (near, far, last):
        total = total + part[...].astype(F32)
    squares = total[:, 4 * RANK :]
    inverse = [
        lax.rsqrt((squares[:, i : i + 1] + squares[:, 3 + i : 4 + i]) / MODEL_WIDTH + EPSILON)
        for i in range(3)
    ]
    mixed = inverse[0] * total[:, :RANK]
    for i in (1, 2):
        mixed = mixed + inverse[i] * total[:, i * RANK : (i + 1) * RANK]
    back = total[:, 3 * RANK : 4 * RANK]
    gate = 1.0 / (1.0 + jnp.exp(-mixed))
    grad = (back * gate * (1.0 + mixed * (1.0 - gate))).astype(BF)
    active = (mixed * gate).astype(BF)
    notes = info[...]
    lane = iota(notes.shape, 1)
    for i in range(3):
        rough = inverse[i].astype(BF).astype(F32)
        notes = jnp.where(lane == i, rough, notes)
        notes = jnp.where(lane == 3 + i, inverse[i] - rough, notes)
    notes = notes.astype(BF)
    for peer in range(out.shape[0]):
        out[peer, :, :RANK] = grad
        out[peer, :, RANK : 2 * RANK] = active
        out[peer, :, 2 * RANK :] = notes


def grads_kernel(place, own, first, second, third, slots, merged, out):
    blocks = slots.shape[1] // RANK
    peer_slots = NX * MOST
    down = [None] * 3
    placed = None
    for k, turned in enumerate((own, first, second, third)):
        source = (place[0] + NX - k) % NX
        rows = jnp.concatenate([merged[2 * source], merged[2 * source + 1]], axis=0)
        notes = rows[:, 2 * RANK :].astype(F32)
        grad = rows[:, :RANK].astype(F32)
        for i in range(3):
            inverse = notes[:, i : i + 1] + notes[:, 3 + i : 4 + i]
            term = dot(turned[i], (inverse * grad).astype(BF))
            down[i] = term if down[i] is None else down[i] + term
        slot = notes[:, 6:7].astype(jnp.int32) * peer_slots + notes[:, 7:8].astype(jnp.int32)
        slot = slot + source * MOST
        chosen = (slot == iota((rows.shape[0], slots.shape[0]), 1)).astype(BF)
        term = dot_tn(rows[:, RANK : 2 * RANK], chosen)
        placed = term if placed is None else placed + term
    for i in range(3):
        out[:, i * RANK : (i + 1) * RANK] = down[i].astype(BF)
    up = dot(placed.astype(BF), slots[...]).astype(BF)
    for b in range(blocks):
        out[b * RANK : (b + 1) * RANK, 3 * RANK :] = up[:, b * RANK : (b + 1) * RANK]


def sum_kernel(parts, out):
    total = parts[0].astype(F32)
    for peer in range(1, parts.shape[0]):
        total = total + parts[peer].astype(F32)
    out[...] = jnp.broadcast_to(total.astype(BF)[None], out.shape)


def final_kernel(parts, down, up):
    for b in range(up.shape[1] // RANK):
        rows = slice(b * RANK, (b + 1) * RANK)
        down[rows, :] = parts[0, b, 0, :, : 3 * RANK].astype(F32)
        up[:, rows] = parts[0, b, 0, :, 3 * RANK :].astype(F32)


def whole(shape):
    return pl.BlockSpec(shape, lambda *_: (0,) * len(shape))


def shape(dims, kind=BF):
    return jax.ShapeDtypeStruct(dims, kind)


def call(kernel, name, out_shape, *args, unread=(), scratch=(), grid=(), limit=32):
    smem = pl.BlockSpec(memory_space=pltpu.SMEM)
    specs = [smem if a.ndim == 1 else whole(a.shape) for a in args]
    specs = specs + [pl.BlockSpec(memory_space=pl.ANY) for _ in unread]
    outs = out_shape if isinstance(out_shape, list) else [out_shape]
    outs = [whole(o.shape) for o in outs]
    return pl.pallas_call(
        kernel,
        grid=grid,
        in_specs=specs,
        out_specs=outs if isinstance(out_shape, list) else outs[0],
        out_shape=out_shape,
        scratch_shapes=[pltpu.VMEM(*s) for s in scratch],
        compiler_params=params(limit),
        cost_estimate=pl.CostEstimate(
            flops=1_000_000, bytes_accessed=2_000_000, transcendentals=0
        ),
        name=name,
    )(*args, *unread)


def body(
    queries,
    tree_keys,
    tree_values,
    cache_keys,
    cache_values,
    parents,
    cache_lengths,
    accepted_counts,
    dest_map,
    low_hidden,
    mid_hidden,
    norm_gains,
    merge_down,
    merge_up,
    out_grad,
):
    count, width = low_hidden.shape
    branches = parents.shape[0]
    nyh, nyl, nzl = lax.axis_size("yh"), lax.axis_size("yl"), lax.axis_size("zl")
    nzh, nc = lax.axis_size("zh"), lax.axis_size("c")
    peers = nyh * nyl * nzl * NX
    block = width // NX
    place = jnp.stack([lax.axis_index("x"), lax.axis_index("c")]).astype(jnp.int32)
    smem = pl.BlockSpec(memory_space=pltpu.SMEM)
    together = 2
    row_block = pl.BlockSpec((together * TREE, width), lambda b: (b, 0))
    cache_block = pl.BlockSpec((together, CACHE, HEAD_DIM), lambda b: (b, 0, 0))

    height = block // RANK * NX * MOST
    everyone = ("yh", "yl", "zl", "x")
    products = call(
        products_kernel,
        "products",
        shape((peers, 8, RANK)),
        out_grad,
        merge_up,
        scratch=[((peers, 8, RANK), F32)],
        grid=(1,),
        limit=60,
    )
    products = lax.all_to_all(products, everyone, 0, 0, tiled=True)
    *turned, partial = pl.pallas_call(
        feature_kernel,
        grid=(branches // together,),
        in_specs=[
            smem,
            smem,
            smem,
            whole((count, 1)),
            whole((branches, TREE)),
            row_block,
            whole((count, HEAD_DIM)),
            whole((count, HEAD_DIM)),
            cache_block,
            cache_block,
            row_block,
            row_block,
            whole((3, width)),
            whole((width, 3 * RANK)),
        ],
        out_specs=[pl.BlockSpec(memory_space=pltpu.HBM)] * NX + [whole((count, 4 * RANK))],
        out_shape=[shape((3, block, count))] * NX + [shape((count, 4 * RANK), F32)],
        scratch_shapes=[
            pltpu.VMEM((count, count), F32),
            pltpu.VMEM((3, count, width), BF),
            pltpu.VMEM((count, RANK), F32),
            pltpu.VMEM((NX, 3, block, count), BF),
            pltpu.SemaphoreType.DMA((NX,)),
        ],
        compiler_params=params(60),
        cost_estimate=pl.CostEstimate(
            flops=400_000_000, bytes_accessed=8_000_000, transcendentals=600_000
        ),
        name="features",
    )(
        place,
        cache_lengths,
        accepted_counts,
        dest_map,
        parents,
        queries,
        tree_keys,
        tree_values,
        cache_keys,
        cache_values,
        low_hidden,
        mid_hidden,
        norm_gains,
        merge_down,
    )
    packed = call(
        pack_kernel,
        "pack",
        shape((peers, height, RANK)),
        out_grad,
        unread=[partial],
        scratch=[((peers, height, RANK), F32)],
        grid=(1,),
        limit=24,
    )
    received = lax.all_to_all(packed, everyone, 0, 0, tiled=True)
    for k in range(1, NX):
        turned[k] = lax.ppermute(turned[k], "x", [(i, (i + k) % NX) for i in range(NX)])
    half = count // nc
    keep, give, info = call(
        pick_kernel,
        "pick",
        [shape((half, 5 * RANK), F32), shape((half, 5 * RANK), F32), shape((half, RANK), F32)],
        products,
        partial,
    )
    got = lax.ppermute(give, "c", [(i, 1 - i) for i in range(nc)])
    own = call(pair_kernel, "pair", shape((half, 5 * RANK)), keep, got, unread=turned[1:2])
    parts = [
        lax.ppermute(own, "zh", [(i, (i + k) % nzh) for i in range(nzh)]) for k in range(1, nzh)
    ]
    merged = call(
        merge_kernel,
        "merge",
        shape((NX * nc, half, 3 * RANK)),
        own,
        *parts,
        info,
        unread=turned[2:],
    )
    merged = lax.all_to_all(merged, ("x", "c"), 0, 0, tiled=True)
    slots = call(
        unpack_kernel,
        "unpack",
        shape((peers * NX * MOST, block)),
        received,
        scratch=[((peers * NX * MOST, block), F32)],
    )
    grads = call(
        grads_kernel, "grads", shape((block, 4 * RANK)), place, *turned, slots, merged
    )
    piece = block // (nzl * nyl * nyh)
    grads = lax.all_to_all(
        grads.reshape(nzl * nyl * nyh, piece, 4 * RANK), ("zl", "yl", "yh"), 0, 0, tiled=True
    )
    grads = call(sum_kernel, "total", shape((nyh, piece, 4 * RANK)), grads)
    rows = nyh * piece
    grads = lax.all_to_all(grads, "yh", 0, 0, tiled=True).reshape(rows, 4 * RANK)
    near = nzl * nyl
    grads = jnp.broadcast_to(grads[None], (near * NX, rows, 4 * RANK))
    grads = lax.all_to_all(grads, ("zl", "yl", "x"), 0, 0, tiled=True)
    grads = grads.reshape(nzl, nyl, NX, rows, 4 * RANK)
    step = nyl * rows
    return pl.pallas_call(
        final_kernel,
        grid=(nzl * NX,),
        in_specs=[
            pl.BlockSpec(
                (1, nyl, 1, rows, 4 * RANK), lambda i: (i % nzl, 0, i // nzl, 0, 0)
            )
        ],
        out_specs=[
            pl.BlockSpec((step, 3 * RANK), lambda i: (i, 0)),
            pl.BlockSpec((RANK, step), lambda i: (0, i)),
        ],
        out_shape=[shape((width, 3 * RANK), F32), shape((RANK, width), F32)],
        compiler_params=params(),
        name="final",
    )(grads)


def solution(mesh):
    fine = Mesh(mesh.devices.reshape(4, 2, 2, NX, 4, 2), ("yh", "yl", "zl", "x", "zh", "c"))
    dp, head = ("yh", "yl", "zl", "x"), ("zh", "c")
    placed = (
        P(dp, head),
        P(dp, head),
        P(dp, head),
        P(dp, None, head),
        P(dp, None, head),
        P(dp, None),
        P(dp),
        P(dp),
        P(dp, None),
        P(dp, head),
        P(dp, head),
        P(None, head),
        P(head, None),
        P(None, head),
        P(dp, head),
    )
    return jax.shard_map(
        body,
        mesh=fine,
        in_specs=placed,
        out_specs=(P(head, None), P(None, head)),
        check_vma=False,
    )
```

```python
import jax
import jax.numpy as jnp
from jax import lax
from jax.experimental import pallas as pl
from jax.experimental.pallas import tpu as pltpu
from jax.sharding import Mesh, PartitionSpec as P

MODEL_WIDTH = 16384
HEAD_DIM = 128
TREE = 16
CACHE = 128
RANK = 128
MOST = 3
NX = 4
PEERS = 64
EPSILON = 1e-05
MASKED = -1e30
BF = jnp.bfloat16
F32 = jnp.float32
MIB = 1024 * 1024


def params(limit=32):
    return pltpu.CompilerParams(vmem_limit_bytes=limit * MIB)


def iota(shape, dim):
    return lax.broadcasted_iota(jnp.int32, shape, dim)


def dot(a, b):
    return jnp.dot(a, b, preferred_element_type=F32)


def dot_nt(a, b):
    return lax.dot_general(a, b, (((1,), (1,)), ((), ())), preferred_element_type=F32)


def dot_tn(a, b):
    return lax.dot_general(a, b, (((0,), (0,)), ((), ())), preferred_element_type=F32)


def feature_kernel(
    place,
    lengths,
    counts,
    targets,
    parents,
    queries,
    tree_keys,
    tree_values,
    cache_keys,
    cache_values,
    low,
    mid,
    gains,
    merge_down,
    own,
    first,
    second,
    third,
    partial,
    reach,
    rows,
    squares,
    turned,
    sent,
):
    together = cache_keys.shape[0]
    count, width = rows.shape[1], rows.shape[2]
    heads = width // HEAD_DIM

    @pl.when(pl.program_id(0) == 0)
    def _():
        groups = parents.shape[0]
        owner = (iota((count, groups), 0) // TREE == iota((count, groups), 1)).astype(F32)
        spread = jnp.dot(owner, parents[...].astype(F32), preferred_element_type=F32)
        same = iota((count, TREE), 0) % TREE == iota((count, TREE), 1)
        parent = jnp.sum(jnp.where(same, spread, 0.0), axis=1, keepdims=True).astype(jnp.int32)
        row, column = iota((count, count), 0), iota((count, count), 1)
        linked = (column == row) | ((parent >= 0) & (column == row // TREE * TREE + parent))
        reached = jnp.where(linked, 1.0, 0.0)
        for _ in range((TREE - 1).bit_length()):
            step = reached.astype(BF)
            reached = jnp.minimum(dot(step, step), 1.0)
        reach[...] = reached

    for j in range(together):
        branch = pl.program_id(0) * together + j
        start = pl.multiple_of(branch * TREE, TREE)
        mine = slice(j * TREE, (j + 1) * TREE)
        here = pl.ds(start, TREE)
        query = queries[mine, :]
        query = jnp.concatenate(
            [query[:, h * HEAD_DIM : (h + 1) * HEAD_DIM] for h in range(heads)], axis=0
        )
        keys = jnp.concatenate([cache_keys[j], tree_keys[...]], axis=0)
        values = jnp.concatenate([cache_values[j], tree_values[...]], axis=0)
        scores = dot_nt(query, keys) * (HEAD_DIM**-0.5)
        live = jnp.where(iota((TREE, CACHE), 1) < lengths[branch], 1.0, 0.0)
        seen = jnp.concatenate([live, reach[here, :]], axis=1) > 0.5
        scores = jnp.where(seen[None], scores.reshape(heads, TREE, CACHE + count), MASKED)
        weights = jnp.exp(scores - jnp.max(scores, axis=2, keepdims=True))
        probs = (weights / jnp.sum(weights, axis=2, keepdims=True)).astype(BF)
        attended = dot(probs.reshape(heads * TREE, CACHE + count), values).astype(BF)
        attended = jnp.concatenate(
            [attended[h * TREE : (h + 1) * TREE, :] for h in range(heads)], axis=1
        )
        kept = iota((TREE, 1), 0) < counts[branch]
        lane = iota((TREE, RANK), 1)
        totals = jnp.zeros((TREE, RANK), F32)
        for layer, feature in enumerate((low[mine, :], mid[mine, :], attended)):
            feature = jnp.where(kept, feature.astype(F32), 0.0)
            total = jnp.sum(feature * feature, axis=1, keepdims=True)
            totals = totals + jnp.where(lane == layer, total, 0.0)
            gain = gains[layer : layer + 1, :].astype(F32)
            rows[layer, here, :] = (feature * gain).astype(BF)
        squares[here, :] = totals

    @pl.when(pl.program_id(0) == pl.num_programs(0) - 1)
    def _():
        block = own.shape[1]
        copies = []
        for k, out in enumerate((own, first, second, third)):
            chunk = (place[0] + k) % (width // block)
            chunk = pl.ds(pl.multiple_of(chunk * block, block), block)
            for layer in range(3):
                turned[k, layer] = rows[layer, :, chunk].T
            copies.append(pltpu.make_async_copy(turned.at[k], out, sent.at[k]))
            copies[k].start()
        for layer in range(3):
            columns = slice(layer * RANK, (layer + 1) * RANK)
            partial[:, columns] = dot(rows[layer], merge_down[:, columns])
        target = targets[...]
        named = (target == iota((count, PEERS), 1)).astype(F32)
        earlier = (iota((count, count), 0) > iota((count, count), 1)).astype(BF)
        rank = jnp.sum(dot(earlier, named.astype(BF)) * named, axis=1, keepdims=True)
        notes = squares[...]
        lane = iota((count, RANK), 1)
        for i, note in ((6, target.astype(F32)), (7, rank)):
            notes = jnp.where(lane == i, note, notes)
        partial[:, 3 * RANK :] = notes
        for copy in copies:
            copy.wait()


def pack_kernel(grads, merge_up, out, rows):
    peers, height = out.shape[0], out.shape[1]
    slots = grads.shape[0] // (peers // NX)
    blocks = grads.shape[1] // NX // RANK
    wide = grads[...].astype(F32)
    products = dot_nt(grads[...], merge_up[...])
    rows[:, blocks * slots :, :] = jnp.zeros((peers, height - blocks * slots, RANK), F32)
    for x in range(NX):
        for b in range(blocks):
            column = (x * blocks + b) * RANK
            for g in range(peers // NX):
                rows[g * NX + x, b * slots : (b + 1) * slots, :] = wide[
                    g * slots : (g + 1) * slots, column : column + RANK
                ]
    for d in range(peers):
        rows[d, blocks * slots : blocks * slots + MOST, :] = products[d * MOST : (d + 1) * MOST, :]
    out[...] = rows[...].astype(BF)


def unpack_kernel(received, out, rows):
    peers = received.shape[0]
    slots = out.shape[0] // peers
    for j in range(peers):
        wide = received[j].astype(F32)
        for b in range(out.shape[1] // RANK):
            rows[j * slots : (j + 1) * slots, b * RANK : (b + 1) * RANK] = wide[
                b * slots : (b + 1) * slots, :
            ]
    out[...] = rows[...].astype(BF)


def pick_kernel(received, partial, out):
    count = partial.shape[0]
    peers = received.shape[0]
    tail = received[:, received.shape[1] - 8 :, :].astype(F32).reshape(peers * 8, RANK).astype(BF)
    notes = partial[:, 3 * RANK :]
    place = (notes[:, 6:7] * 8.0 + notes[:, 7:8]).astype(jnp.int32)
    chosen = place == iota((count, peers * 8), 1)
    out[:, : 3 * RANK] = partial[:, : 3 * RANK].astype(BF)
    out[:, 3 * RANK : 4 * RANK] = dot(chosen.astype(BF), tail).astype(BF)
    rough = notes.astype(BF).astype(F32)
    lane = iota(notes.shape, 1)
    for i in range(3):
        rest = notes[:, i : i + 1] - rough[:, i : i + 1]
        rough = jnp.where(lane == 3 + i, rest, rough)
    out[:, 4 * RANK :] = rough.astype(BF)


def merge_kernel(parts, *refs):
    out = refs[-1]
    total = parts[0].astype(F32)
    for peer in range(1, parts.shape[0]):
        total = total + parts[peer].astype(F32)
    squares = total[:, 4 * RANK :]
    inverse = [
        lax.rsqrt((squares[:, i : i + 1] + squares[:, 3 + i : 4 + i]) / MODEL_WIDTH + EPSILON)
        for i in range(3)
    ]
    mixed = inverse[0] * total[:, :RANK]
    for i in (1, 2):
        mixed = mixed + inverse[i] * total[:, i * RANK : (i + 1) * RANK]
    back = total[:, 3 * RANK : 4 * RANK]
    gate = 1.0 / (1.0 + jnp.exp(-mixed))
    grad = (back * gate * (1.0 + mixed * (1.0 - gate))).astype(BF)
    active = (mixed * gate).astype(BF)
    notes = squares / parts.shape[0]
    lane = iota(notes.shape, 1)
    for i in range(3):
        rough = inverse[i].astype(BF).astype(F32)
        notes = jnp.where(lane == i, rough, notes)
        notes = jnp.where(lane == 3 + i, inverse[i] - rough, notes)
    notes = notes.astype(BF)
    for peer in range(out.shape[0]):
        out[peer, :, :RANK] = grad
        out[peer, :, RANK : 2 * RANK] = active
        out[peer, :, 2 * RANK :] = notes


def grads_kernel(place, own, first, second, third, slots, merged, out):
    blocks = slots.shape[1] // RANK
    peer_slots = NX * MOST
    down = [None] * 3
    placed = None
    for k, turned in enumerate((own, first, second, third)):
        source = (place[0] + NX - k) % NX
        rows = merged[source]
        notes = rows[:, 2 * RANK :].astype(F32)
        grad = rows[:, :RANK].astype(F32)
        for i in range(3):
            inverse = notes[:, i : i + 1] + notes[:, 3 + i : 4 + i]
            term = dot(turned[i], (inverse * grad).astype(BF))
            down[i] = term if down[i] is None else down[i] + term
        slot = notes[:, 6:7].astype(jnp.int32) * peer_slots + notes[:, 7:8].astype(jnp.int32)
        slot = slot + source * MOST
        chosen = (slot == iota((rows.shape[0], slots.shape[0]), 1)).astype(BF)
        term = dot_tn(rows[:, RANK : 2 * RANK], chosen)
        placed = term if placed is None else placed + term
    for i in range(3):
        out[:, i * RANK : (i + 1) * RANK] = down[i].astype(BF)
    up = dot(placed.astype(BF), slots[...]).astype(BF)
    for b in range(blocks):
        out[b * RANK : (b + 1) * RANK, 3 * RANK :] = up[:, b * RANK : (b + 1) * RANK]


def sum_kernel(parts, out):
    total = parts[0].astype(F32)
    for peer in range(1, parts.shape[0]):
        total = total + parts[peer].astype(F32)
    out[...] = jnp.broadcast_to(total.astype(BF)[None], out.shape)


def final_kernel(parts, down, up):
    for b in range(up.shape[1] // RANK):
        rows = slice(b * RANK, (b + 1) * RANK)
        down[rows, :] = parts[0, b, 0, :, : 3 * RANK].astype(F32)
        up[:, rows] = parts[0, b, 0, :, 3 * RANK :].astype(F32)


def whole(shape):
    return pl.BlockSpec(shape, lambda *_: (0,) * len(shape))


def shape(dims, kind=BF):
    return jax.ShapeDtypeStruct(dims, kind)


def call(kernel, name, out_shape, *args, unread=(), scratch=(), grid=(), limit=32):
    smem = pl.BlockSpec(memory_space=pltpu.SMEM)
    specs = [smem if a.ndim == 1 else whole(a.shape) for a in args]
    specs = specs + [pl.BlockSpec(memory_space=pl.ANY) for _ in unread]
    outs = out_shape if isinstance(out_shape, list) else [out_shape]
    outs = [whole(o.shape) for o in outs]
    return pl.pallas_call(
        kernel,
        grid=grid,
        in_specs=specs,
        out_specs=outs if isinstance(out_shape, list) else outs[0],
        out_shape=out_shape,
        scratch_shapes=[pltpu.VMEM(*s) for s in scratch],
        compiler_params=params(limit),
        cost_estimate=pl.CostEstimate(
            flops=1_000_000, bytes_accessed=2_000_000, transcendentals=0
        ),
        name=name,
    )(*args, *unread)


def body(
    queries,
    tree_keys,
    tree_values,
    cache_keys,
    cache_values,
    parents,
    cache_lengths,
    accepted_counts,
    dest_map,
    low_hidden,
    mid_hidden,
    norm_gains,
    merge_down,
    merge_up,
    out_grad,
):
    count, width = low_hidden.shape
    branches = parents.shape[0]
    nyh, nyl, nzl = lax.axis_size("yh"), lax.axis_size("yl"), lax.axis_size("zl")
    nzh, nc = lax.axis_size("zh"), lax.axis_size("c")
    peers = nyh * nyl * nzl * NX
    block = width // NX
    place = lax.axis_index("x").astype(jnp.int32).reshape(1)
    smem = pl.BlockSpec(memory_space=pltpu.SMEM)
    together = 2
    row_block = pl.BlockSpec((together * TREE, width), lambda b: (b, 0))
    cache_block = pl.BlockSpec((together, CACHE, HEAD_DIM), lambda b: (b, 0, 0))

    height = block // RANK * NX * MOST + 8
    packed = call(
        pack_kernel,
        "pack",
        shape((peers, height, RANK)),
        out_grad,
        merge_up,
        scratch=[((peers, height, RANK), F32)],
        grid=(1,),
        limit=60,
    )
    received = lax.all_to_all(packed, ("yh", "yl", "zl", "x"), 0, 0, tiled=True)
    *turned, partial = pl.pallas_call(
        feature_kernel,
        grid=(branches // together,),
        in_specs=[
            smem,
            smem,
            smem,
            whole((count, 1)),
            whole((branches, TREE)),
            row_block,
            whole((count, HEAD_DIM)),
            whole((count, HEAD_DIM)),
            cache_block,
            cache_block,
            row_block,
            row_block,
            whole((3, width)),
            whole((width, 3 * RANK)),
        ],
        out_specs=[pl.BlockSpec(memory_space=pltpu.HBM)] * NX + [whole((count, 4 * RANK))],
        out_shape=[shape((3, block, count))] * NX + [shape((count, 4 * RANK), F32)],
        scratch_shapes=[
            pltpu.VMEM((count, count), F32),
            pltpu.VMEM((3, count, width), BF),
            pltpu.VMEM((count, RANK), F32),
            pltpu.VMEM((NX, 3, block, count), BF),
            pltpu.SemaphoreType.DMA((NX,)),
        ],
        compiler_params=params(60),
        cost_estimate=pl.CostEstimate(
            flops=400_000_000, bytes_accessed=8_000_000, transcendentals=600_000
        ),
        name="features",
    )(
        place,
        cache_lengths,
        accepted_counts,
        dest_map,
        parents,
        queries,
        tree_keys,
        tree_values,
        cache_keys,
        cache_values,
        low_hidden,
        mid_hidden,
        norm_gains,
        merge_down,
    )
    for k in range(1, NX):
        turned[k] = lax.ppermute(turned[k], "x", [(i, (i + k) % NX) for i in range(NX)])
    sent = call(pick_kernel, "pick", shape((count, 5 * RANK)), received, partial)
    share = count // (nzh * nc)
    parts = lax.all_to_all(sent.reshape(nzh * nc, share, 5 * RANK), ("zh", "c"), 0, 0, tiled=True)
    merged = call(
        merge_kernel,
        "merge",
        shape((NX * nzh * nc, share, 3 * RANK)),
        parts,
        unread=turned[1:],
    )
    merged = lax.all_to_all(merged, ("x", "zh", "c"), 0, 0, tiled=True)
    merged = merged.reshape(NX, count, 3 * RANK)
    slots = call(
        unpack_kernel,
        "unpack",
        shape((peers * NX * MOST, block)),
        received,
        scratch=[((peers * NX * MOST, block), F32)],
    )
    grads = call(
        grads_kernel, "grads", shape((block, 4 * RANK)), place, *turned, slots, merged
    )
    piece = block // (nzl * nyl * nyh)
    grads = lax.all_to_all(
        grads.reshape(nzl * nyl * nyh, piece, 4 * RANK), ("zl", "yl", "yh"), 0, 0, tiled=True
    )
    grads = call(sum_kernel, "total", shape((nyh, piece, 4 * RANK)), grads)
    rows = nyh * piece
    grads = lax.all_to_all(grads, "yh", 0, 0, tiled=True).reshape(rows, 4 * RANK)
    near = nzl * nyl
    grads = jnp.broadcast_to(grads[None], (near * NX, rows, 4 * RANK))
    grads = lax.all_to_all(grads, ("zl", "yl", "x"), 0, 0, tiled=True)
    grads = grads.reshape(nzl, nyl, NX, rows, 4 * RANK)
    step = nyl * rows
    return pl.pallas_call(
        final_kernel,
        grid=(nzl * NX,),
        in_specs=[
            pl.BlockSpec(
                (1, nyl, 1, rows, 4 * RANK), lambda i: (i % nzl, 0, i // nzl, 0, 0)
            )
        ],
        out_specs=[
            pl.BlockSpec((step, 3 * RANK), lambda i: (i, 0)),
            pl.BlockSpec((RANK, step), lambda i: (0, i)),
        ],
        out_shape=[shape((width, 3 * RANK), F32), shape((RANK, width), F32)],
        compiler_params=params(),
        name="final",
    )(grads)


def solution(mesh):
    fine = Mesh(mesh.devices.reshape(4, 2, 2, NX, 4, 2), ("yh", "yl", "zl", "x", "zh", "c"))
    dp, head = ("yh", "yl", "zl", "x"), ("zh", "c")
    placed = (
        P(dp, head),
        P(dp, head),
        P(dp, head),
        P(dp, None, head),
        P(dp, None, head),
        P(dp, None),
        P(dp),
        P(dp),
        P(dp, None),
        P(dp, head),
        P(dp, head),
        P(None, head),
        P(head, None),
        P(None, head),
        P(dp, head),
    )
    return jax.shard_map(
        body,
        mesh=fine,
        in_specs=placed,
        out_specs=(P(head, None), P(None, head)),
        check_vma=False,
    )
```

```python
import jax
import jax.numpy as jnp
from jax import lax
from jax.experimental import pallas as pl
from jax.experimental.pallas import tpu as pltpu
from jax.sharding import Mesh, PartitionSpec as P

MODEL_WIDTH = 16384
HEAD_DIM = 128
TREE = 16
CACHE = 128
RANK = 128
MOST = 3
NX = 4
PEERS = 64
EPSILON = 1e-05
MASKED = -1e30
BF = jnp.bfloat16
F32 = jnp.float32
MIB = 1024 * 1024


def params(limit=32):
    return pltpu.CompilerParams(vmem_limit_bytes=limit * MIB)


def iota(shape, dim):
    return lax.broadcasted_iota(jnp.int32, shape, dim)


def dot(a, b):
    return jnp.dot(a, b, preferred_element_type=F32)


def dot_nt(a, b):
    return lax.dot_general(a, b, (((1,), (1,)), ((), ())), preferred_element_type=F32)


def dot_tn(a, b):
    return lax.dot_general(a, b, (((0,), (0,)), ((), ())), preferred_element_type=F32)


def feature_kernel(
    place,
    lengths,
    counts,
    targets,
    parents,
    queries,
    tree_keys,
    tree_values,
    cache_keys,
    cache_values,
    low,
    mid,
    gains,
    merge_down,
    own,
    first,
    second,
    third,
    partial,
    reach,
    rows,
    squares,
    turned,
    sent,
):
    together = cache_keys.shape[0]
    count, width = rows.shape[1], rows.shape[2]
    heads = width // HEAD_DIM

    @pl.when(pl.program_id(0) == 0)
    def _():
        groups = parents.shape[0]
        owner = (iota((count, groups), 0) // TREE == iota((count, groups), 1)).astype(F32)
        spread = jnp.dot(owner, parents[...].astype(F32), preferred_element_type=F32)
        same = iota((count, TREE), 0) % TREE == iota((count, TREE), 1)
        parent = jnp.sum(jnp.where(same, spread, 0.0), axis=1, keepdims=True).astype(jnp.int32)
        row, column = iota((count, count), 0), iota((count, count), 1)
        linked = (column == row) | ((parent >= 0) & (column == row // TREE * TREE + parent))
        reached = jnp.where(linked, 1.0, 0.0)
        for _ in range((TREE - 1).bit_length()):
            step = reached.astype(BF)
            reached = jnp.minimum(dot(step, step), 1.0)
        reach[...] = reached

    for j in range(together):
        branch = pl.program_id(0) * together + j
        start = pl.multiple_of(branch * TREE, TREE)
        mine = slice(j * TREE, (j + 1) * TREE)
        here = pl.ds(start, TREE)
        query = queries[mine, :]
        query = jnp.concatenate(
            [query[:, h * HEAD_DIM : (h + 1) * HEAD_DIM] for h in range(heads)], axis=0
        )
        keys = jnp.concatenate([cache_keys[j], tree_keys[...]], axis=0)
        values = jnp.concatenate([cache_values[j], tree_values[...]], axis=0)
        scores = dot_nt(query, keys) * (HEAD_DIM**-0.5)
        live = jnp.where(iota((TREE, CACHE), 1) < lengths[branch], 1.0, 0.0)
        seen = jnp.concatenate([live, reach[here, :]], axis=1) > 0.5
        scores = jnp.where(seen[None], scores.reshape(heads, TREE, CACHE + count), MASKED)
        weights = jnp.exp(scores - jnp.max(scores, axis=2, keepdims=True))
        probs = (weights / jnp.sum(weights, axis=2, keepdims=True)).astype(BF)
        attended = dot(probs.reshape(heads * TREE, CACHE + count), values).astype(BF)
        attended = jnp.concatenate(
            [attended[h * TREE : (h + 1) * TREE, :] for h in range(heads)], axis=1
        )
        kept = iota((TREE, 1), 0) < counts[branch]
        lane = iota((TREE, RANK), 1)
        totals = jnp.zeros((TREE, RANK), F32)
        for layer, feature in enumerate((low[mine, :], mid[mine, :], attended)):
            feature = jnp.where(kept, feature.astype(F32), 0.0)
            total = jnp.sum(feature * feature, axis=1, keepdims=True)
            totals = totals + jnp.where(lane == layer, total, 0.0)
            gain = gains[layer : layer + 1, :].astype(F32)
            rows[layer, here, :] = (feature * gain).astype(BF)
        squares[here, :] = totals

    @pl.when(pl.program_id(0) == pl.num_programs(0) - 1)
    def _():
        block = own.shape[1]
        copies = []
        for k, out in enumerate((own, first, second, third)):
            chunk = (place[0] + k) % (width // block)
            chunk = pl.ds(pl.multiple_of(chunk * block, block), block)
            for layer in range(3):
                turned[k, layer] = rows[layer, :, chunk].T
            copies.append(pltpu.make_async_copy(turned.at[k], out, sent.at[k]))
            copies[k].start()
        for layer in range(3):
            columns = slice(layer * RANK, (layer + 1) * RANK)
            partial[:, columns] = dot(rows[layer], merge_down[:, columns])
        target = targets[...]
        named = (target == iota((count, PEERS), 1)).astype(F32)
        earlier = (iota((count, count), 0) > iota((count, count), 1)).astype(BF)
        rank = jnp.sum(dot(earlier, named.astype(BF)) * named, axis=1, keepdims=True)
        notes = squares[...]
        lane = iota((count, RANK), 1)
        for i, note in ((6, target.astype(F32)), (7, rank)):
            notes = jnp.where(lane == i, note, notes)
        partial[:, 3 * RANK :] = notes
        for copy in copies:
            copy.wait()


def pack_kernel(grads, merge_up, out, rows):
    peers, height = out.shape[0], out.shape[1]
    slots = grads.shape[0] // (peers // NX)
    blocks = grads.shape[1] // NX // RANK
    wide = grads[...].astype(F32)
    products = dot_nt(grads[...], merge_up[...])
    rows[:, blocks * slots :, :] = jnp.zeros((peers, height - blocks * slots, RANK), F32)
    for x in range(NX):
        for b in range(blocks):
            column = (x * blocks + b) * RANK
            for g in range(peers // NX):
                rows[g * NX + x, b * slots : (b + 1) * slots, :] = wide[
                    g * slots : (g + 1) * slots, column : column + RANK
                ]
    for d in range(peers):
        rows[d, blocks * slots : blocks * slots + MOST, :] = products[d * MOST : (d + 1) * MOST, :]
    out[...] = rows[...].astype(BF)


def unpack_kernel(received, out, rows):
    peers = received.shape[0]
    slots = out.shape[0] // peers
    for j in range(peers):
        wide = received[j].astype(F32)
        for b in range(out.shape[1] // RANK):
            rows[j * slots : (j + 1) * slots, b * RANK : (b + 1) * RANK] = wide[
                b * slots : (b + 1) * slots, :
            ]
    out[...] = rows[...].astype(BF)


def ready_kernel(partial, base, chosen):
    notes = partial[:, 3 * RANK :]
    place = (notes[:, 6:7] * 8.0 + notes[:, 7:8]).astype(jnp.int32)
    chosen[...] = (place == iota(chosen.shape, 1)).astype(BF)
    base[:, : 3 * RANK] = partial[:, : 3 * RANK].astype(BF)
    rough = notes.astype(BF).astype(F32)
    lane = iota(notes.shape, 1)
    for i in range(3):
        rest = notes[:, i : i + 1] - rough[:, i : i + 1]
        rough = jnp.where(lane == 3 + i, rest, rough)
    base[:, 3 * RANK :] = rough.astype(BF)


def pick_kernel(received, base, chosen, out):
    peers = received.shape[0]
    tail = received[:, received.shape[1] - 8 :, :].astype(F32).reshape(peers * 8, RANK).astype(BF)
    out[:, : 3 * RANK] = base[:, : 3 * RANK]
    out[:, 3 * RANK : 4 * RANK] = dot(chosen[...], tail).astype(BF)
    out[:, 4 * RANK :] = base[:, 3 * RANK :]


def merge_kernel(parts, *refs):
    out = refs[-1]
    total = parts[0].astype(F32)
    for peer in range(1, parts.shape[0]):
        total = total + parts[peer].astype(F32)
    squares = total[:, 4 * RANK :]
    inverse = [
        lax.rsqrt((squares[:, i : i + 1] + squares[:, 3 + i : 4 + i]) / MODEL_WIDTH + EPSILON)
        for i in range(3)
    ]
    mixed = inverse[0] * total[:, :RANK]
    for i in (1, 2):
        mixed = mixed + inverse[i] * total[:, i * RANK : (i + 1) * RANK]
    back = total[:, 3 * RANK : 4 * RANK]
    gate = 1.0 / (1.0 + jnp.exp(-mixed))
    grad = (back * gate * (1.0 + mixed * (1.0 - gate))).astype(BF)
    active = (mixed * gate).astype(BF)
    notes = squares / parts.shape[0]
    lane = iota(notes.shape, 1)
    for i in range(3):
        rough = inverse[i].astype(BF).astype(F32)
        notes = jnp.where(lane == i, rough, notes)
        notes = jnp.where(lane == 3 + i, inverse[i] - rough, notes)
    notes = notes.astype(BF)
    for peer in range(out.shape[0]):
        out[peer, :, :RANK] = grad
        out[peer, :, RANK : 2 * RANK] = active
        out[peer, :, 2 * RANK :] = notes


def grads_kernel(place, own, first, second, third, slots, merged, out):
    blocks = slots.shape[1] // RANK
    peer_slots = NX * MOST
    down = [None] * 3
    placed = None
    for k, turned in enumerate((own, first, second, third)):
        source = (place[0] + NX - k) % NX
        rows = merged[source]
        notes = rows[:, 2 * RANK :].astype(F32)
        grad = rows[:, :RANK].astype(F32)
        for i in range(3):
            inverse = notes[:, i : i + 1] + notes[:, 3 + i : 4 + i]
            term = dot(turned[i], (inverse * grad).astype(BF))
            down[i] = term if down[i] is None else down[i] + term
        slot = notes[:, 6:7].astype(jnp.int32) * peer_slots + notes[:, 7:8].astype(jnp.int32)
        slot = slot + source * MOST
        chosen = (slot == iota((rows.shape[0], slots.shape[0]), 1)).astype(BF)
        term = dot_tn(rows[:, RANK : 2 * RANK], chosen)
        placed = term if placed is None else placed + term
    for i in range(3):
        out[:, i * RANK : (i + 1) * RANK] = down[i].astype(BF)
    up = dot(placed.astype(BF), slots[...]).astype(BF)
    for b in range(blocks):
        out[b * RANK : (b + 1) * RANK, 3 * RANK :] = up[:, b * RANK : (b + 1) * RANK]


def sum_kernel(parts, out):
    total = parts[0].astype(F32)
    for peer in range(1, parts.shape[0]):
        total = total + parts[peer].astype(F32)
    out[...] = jnp.broadcast_to(total.astype(BF)[None], out.shape)


def final_kernel(parts, down, up):
    piece = parts.shape[3]
    for y in range(parts.shape[2]):
        for z in range(parts.shape[0]):
            start = (y * parts.shape[0] + z) * piece
            block, rank = start // RANK, start % RANK
            down[start : start + piece, :] = parts[z, 0, y, :, : 3 * RANK].astype(F32)
            up[rank : rank + piece, block * RANK : (block + 1) * RANK] = parts[
                z, 0, y, :, 3 * RANK :
            ].astype(F32)


def whole(shape):
    return pl.BlockSpec(shape, lambda *_: (0,) * len(shape))


def shape(dims, kind=BF):
    return jax.ShapeDtypeStruct(dims, kind)


def call(kernel, name, out_shape, *args, unread=(), scratch=(), grid=(), limit=32):
    smem = pl.BlockSpec(memory_space=pltpu.SMEM)
    specs = [smem if a.ndim == 1 else whole(a.shape) for a in args]
    specs = specs + [pl.BlockSpec(memory_space=pl.ANY) for _ in unread]
    outs = out_shape if isinstance(out_shape, list) else [out_shape]
    outs = [whole(o.shape) for o in outs]
    return pl.pallas_call(
        kernel,
        grid=grid,
        in_specs=specs,
        out_specs=outs if isinstance(out_shape, list) else outs[0],
        out_shape=out_shape,
        scratch_shapes=[pltpu.VMEM(*s) for s in scratch],
        compiler_params=params(limit),
        cost_estimate=pl.CostEstimate(
            flops=1_000_000, bytes_accessed=2_000_000, transcendentals=0
        ),
        name=name,
    )(*args, *unread)


def body(
    queries,
    tree_keys,
    tree_values,
    cache_keys,
    cache_values,
    parents,
    cache_lengths,
    accepted_counts,
    dest_map,
    low_hidden,
    mid_hidden,
    norm_gains,
    merge_down,
    merge_up,
    out_grad,
):
    count, width = low_hidden.shape
    branches = parents.shape[0]
    ny, nzl, nh = lax.axis_size("y"), lax.axis_size("zl"), lax.axis_size("head")
    peers = ny * nzl * NX
    block = width // NX
    place = lax.axis_index("x").astype(jnp.int32).reshape(1)
    smem = pl.BlockSpec(memory_space=pltpu.SMEM)
    together = 2
    row_block = pl.BlockSpec((together * TREE, width), lambda b: (b, 0))
    cache_block = pl.BlockSpec((together, CACHE, HEAD_DIM), lambda b: (b, 0, 0))

    height = block // RANK * NX * MOST + 8
    steps = 4
    some = peers // steps
    packed = pl.pallas_call(
        pack_kernel,
        grid=(steps,),
        in_specs=[
            pl.BlockSpec((out_grad.shape[0] // steps, width), lambda i: (i, 0)),
            whole(merge_up.shape),
        ],
        out_specs=pl.BlockSpec((some, height, RANK), lambda i: (i, 0, 0)),
        out_shape=shape((peers, height, RANK)),
        scratch_shapes=[pltpu.VMEM((some, height, RANK), F32)],
        compiler_params=params(60),
        name="pack",
    )(out_grad, merge_up)
    received = lax.all_to_all(packed, ("y", "zl", "x"), 0, 0, tiled=True)
    *turned, partial = pl.pallas_call(
        feature_kernel,
        grid=(branches // together,),
        in_specs=[
            smem,
            smem,
            smem,
            whole((count, 1)),
            whole((branches, TREE)),
            row_block,
            whole((count, HEAD_DIM)),
            whole((count, HEAD_DIM)),
            cache_block,
            cache_block,
            row_block,
            row_block,
            whole((3, width)),
            whole((width, 3 * RANK)),
        ],
        out_specs=[pl.BlockSpec(memory_space=pltpu.HBM)] * NX + [whole((count, 4 * RANK))],
        out_shape=[shape((3, block, count))] * NX + [shape((count, 4 * RANK), F32)],
        scratch_shapes=[
            pltpu.VMEM((count, count), F32),
            pltpu.VMEM((3, count, width), BF),
            pltpu.VMEM((count, RANK), F32),
            pltpu.VMEM((NX, 3, block, count), BF),
            pltpu.SemaphoreType.DMA((NX,)),
        ],
        compiler_params=params(60),
        cost_estimate=pl.CostEstimate(
            flops=400_000_000, bytes_accessed=8_000_000, transcendentals=600_000
        ),
        name="features",
    )(
        place,
        cache_lengths,
        accepted_counts,
        dest_map,
        parents,
        queries,
        tree_keys,
        tree_values,
        cache_keys,
        cache_values,
        low_hidden,
        mid_hidden,
        norm_gains,
        merge_down,
    )
    for k in range(1, NX):
        turned[k] = lax.ppermute(turned[k], "x", [(i, (i + k) % NX) for i in range(NX)])
    base, chosen = call(
        ready_kernel, "ready", [shape((count, 4 * RANK)), shape((count, peers * 8))], partial
    )
    sent = call(pick_kernel, "pick", shape((count, 5 * RANK)), received, base, chosen)
    share = count // nh
    parts = lax.all_to_all(sent.reshape(nh, share, 5 * RANK), "head", 0, 0, tiled=True)
    merged = call(
        merge_kernel,
        "merge",
        shape((NX * nh, share, 3 * RANK)),
        parts,
        unread=turned[1:],
    )
    merged = lax.all_to_all(merged, ("x", "head"), 0, 0, tiled=True)
    merged = merged.reshape(NX, count, 3 * RANK)
    slots = call(
        unpack_kernel,
        "unpack",
        shape((peers * NX * MOST, block)),
        received,
        scratch=[((peers * NX * MOST, block), F32)],
    )
    grads = call(grads_kernel, "grads", shape((block, 4 * RANK)), place, *turned, slots, merged)
    piece = block // (ny * nzl)
    grads = lax.all_to_all(
        grads.reshape(ny * nzl, piece, 4 * RANK), ("y", "zl"), 0, 0, tiled=True
    )
    return call(sum_kernel, "total", shape((ny, piece, 4 * RANK)), grads)


def gather(grads, width):
    ny, piece, lanes = grads.shape
    nzx = lax.axis_size("zx")
    nzl = nzx // NX
    grads = lax.all_to_all(grads, "y", 0, 0, tiled=True).reshape(ny * piece, lanes)
    grads = jnp.broadcast_to(grads[None], (nzx, ny * piece, lanes))
    grads = lax.all_to_all(grads, "zx", 0, 0, tiled=True)
    grads = grads.reshape(nzl, NX, ny, piece, lanes)
    part = 2
    few = ny // part
    rows = few * nzl * piece
    return pl.pallas_call(
        final_kernel,
        grid=(NX * part,),
        in_specs=[
            pl.BlockSpec(
                (nzl, 1, few, piece, lanes), lambda i: (0, i // part, i % part, 0, 0)
            )
        ],
        out_specs=[
            pl.BlockSpec((rows, 3 * RANK), lambda i: (i, 0)),
            pl.BlockSpec((RANK, rows), lambda i: (0, i)),
        ],
        out_shape=[shape((width, 3 * RANK), F32), shape((RANK, width), F32)],
        compiler_params=params(),
        name="final",
    )(grads)


def solution(mesh):
    fine = Mesh(mesh.devices.reshape(8, 2, NX, 8), ("y", "zl", "x", "head"))
    coarse = Mesh(mesh.devices.reshape(8, 2 * NX, 8), ("y", "zx", "head"))
    dp, head = ("y", "zl", "x"), "head"
    placed = (
        P(dp, head),
        P(dp, head),
        P(dp, head),
        P(dp, None, head),
        P(dp, None, head),
        P(dp, None),
        P(dp),
        P(dp),
        P(dp, None),
        P(dp, head),
        P(dp, head),
        P(None, head),
        P(head, None),
        P(None, head),
        P(dp, head),
    )
    own_sums = jax.shard_map(
        body, mesh=fine, in_specs=placed, out_specs=P((*dp, head)), check_vma=False
    )

    def whole_program(*args):
        width = args[9].shape[1] // mesh.shape["head"]
        return jax.shard_map(
            lambda sums: tuple(gather(sums, width)),
            mesh=coarse,
            in_specs=P(("y", "zx", "head")),
            out_specs=(P("head", None), P(None, "head")),
            check_vma=False,
        )(own_sums(*args))

    return whole_program
```

```python
import jax
import jax.numpy as jnp
from jax import lax
from jax.experimental import pallas as pl
from jax.experimental.pallas import tpu as pltpu
from jax.sharding import Mesh, PartitionSpec as P

MODEL_WIDTH = 16384
HEAD_DIM = 128
TREE = 16
CACHE = 128
RANK = 128
MOST = 3
NX = 4
PEERS = 64
EPSILON = 1e-05
MASKED = -1e30
BF = jnp.bfloat16
F32 = jnp.float32
MIB = 1024 * 1024


def params(limit=32):
    return pltpu.CompilerParams(vmem_limit_bytes=limit * MIB)


def iota(shape, dim):
    return lax.broadcasted_iota(jnp.int32, shape, dim)


def dot(a, b):
    return jnp.dot(a, b, preferred_element_type=F32)


def dot_nt(a, b):
    return lax.dot_general(a, b, (((1,), (1,)), ((), ())), preferred_element_type=F32)


def dot_tn(a, b):
    return lax.dot_general(a, b, (((0,), (0,)), ((), ())), preferred_element_type=F32)


def feature_kernel(
    place,
    lengths,
    counts,
    targets,
    parents,
    queries,
    tree_keys,
    tree_values,
    cache_keys,
    cache_values,
    low,
    mid,
    gains,
    merge_down,
    own,
    first,
    second,
    third,
    partial,
    reach,
    rows,
    squares,
    turned,
    sent,
):
    together = cache_keys.shape[0]
    count, width = rows.shape[1], rows.shape[2]
    heads = width // HEAD_DIM

    @pl.when(pl.program_id(0) == 0)
    def _():
        groups = parents.shape[0]
        owner = (iota((count, groups), 0) // TREE == iota((count, groups), 1)).astype(F32)
        spread = jnp.dot(owner, parents[...].astype(F32), preferred_element_type=F32)
        same = iota((count, TREE), 0) % TREE == iota((count, TREE), 1)
        parent = jnp.sum(jnp.where(same, spread, 0.0), axis=1, keepdims=True).astype(jnp.int32)
        row, column = iota((count, count), 0), iota((count, count), 1)
        linked = (column == row) | ((parent >= 0) & (column == row // TREE * TREE + parent))
        reached = jnp.where(linked, 1.0, 0.0)
        for _ in range((TREE - 1).bit_length()):
            step = reached.astype(BF)
            reached = jnp.minimum(dot(step, step), 1.0)
        reach[...] = reached

    for j in range(together):
        branch = pl.program_id(0) * together + j
        start = pl.multiple_of(branch * TREE, TREE)
        mine = slice(j * TREE, (j + 1) * TREE)
        here = pl.ds(start, TREE)
        query = queries[mine, :]
        query = jnp.concatenate(
            [query[:, h * HEAD_DIM : (h + 1) * HEAD_DIM] for h in range(heads)], axis=0
        )
        keys = jnp.concatenate([cache_keys[j], tree_keys[...]], axis=0)
        values = jnp.concatenate([cache_values[j], tree_values[...]], axis=0)
        scores = dot_nt(query, keys) * (HEAD_DIM**-0.5)
        live = jnp.where(iota((TREE, CACHE), 1) < lengths[branch], 1.0, 0.0)
        seen = jnp.concatenate([live, reach[here, :]], axis=1) > 0.5
        scores = jnp.where(seen[None], scores.reshape(heads, TREE, CACHE + count), MASKED)
        weights = jnp.exp(scores - jnp.max(scores, axis=2, keepdims=True))
        probs = (weights / jnp.sum(weights, axis=2, keepdims=True)).astype(BF)
        attended = dot(probs.reshape(heads * TREE, CACHE + count), values).astype(BF)
        attended = jnp.concatenate(
            [attended[h * TREE : (h + 1) * TREE, :] for h in range(heads)], axis=1
        )
        kept = iota((TREE, 1), 0) < counts[branch]
        lane = iota((TREE, RANK), 1)
        totals = jnp.zeros((TREE, RANK), F32)
        for layer, feature in enumerate((low[mine, :], mid[mine, :], attended)):
            feature = jnp.where(kept, feature.astype(F32), 0.0)
            total = jnp.sum(feature * feature, axis=1, keepdims=True)
            totals = totals + jnp.where(lane == layer, total, 0.0)
            gain = gains[layer : layer + 1, :].astype(F32)
            rows[layer, here, :] = (feature * gain).astype(BF)
        squares[here, :] = totals

    @pl.when(pl.program_id(0) == pl.num_programs(0) - 1)
    def _():
        block = own.shape[1]
        copies = []
        for k, out in enumerate((own, first, second, third)):
            chunk = (place[0] + k) % (width // block)
            chunk = pl.ds(pl.multiple_of(chunk * block, block), block)
            for layer in range(3):
                turned[k, layer] = rows[layer, :, chunk].T
            copies.append(pltpu.make_async_copy(turned.at[k], out, sent.at[k]))
            copies[k].start()
        for layer in range(3):
            columns = slice(layer * RANK, (layer + 1) * RANK)
            partial[:, columns] = dot(rows[layer], merge_down[:, columns])
        target = targets[...]
        named = (target == iota((count, PEERS), 1)).astype(F32)
        earlier = (iota((count, count), 0) > iota((count, count), 1)).astype(BF)
        rank = jnp.sum(dot(earlier, named.astype(BF)) * named, axis=1, keepdims=True)
        notes = squares[...]
        lane = iota((count, RANK), 1)
        for i, note in ((6, target.astype(F32)), (7, rank)):
            notes = jnp.where(lane == i, note, notes)
        partial[:, 3 * RANK :] = notes
        for copy in copies:
            copy.wait()


def pack_kernel(grads, merge_up, out, rows):
    peers, height = out.shape[0], out.shape[1]
    slots = grads.shape[0] // (peers // NX)
    blocks = grads.shape[1] // NX // RANK
    wide = grads[...].astype(F32)
    products = dot_nt(grads[...], merge_up[...])
    rows[:, blocks * slots :, :] = jnp.zeros((peers, height - blocks * slots, RANK), F32)
    for x in range(NX):
        for b in range(blocks):
            column = (x * blocks + b) * RANK
            for g in range(peers // NX):
                rows[g * NX + x, b * slots : (b + 1) * slots, :] = wide[
                    g * slots : (g + 1) * slots, column : column + RANK
                ]
    for d in range(peers):
        rows[d, blocks * slots : blocks * slots + MOST, :] = products[d * MOST : (d + 1) * MOST, :]
    out[...] = rows[...].astype(BF)


def unpack_kernel(received, own, first, second, third, out, rows):
    peers = received.shape[0]
    count, block = rows.shape
    slots = count // peers
    for j in range(peers):
        wide = received[j].astype(F32)
        for b in range(block // RANK):
            rows[j * slots : (j + 1) * slots, b * RANK : (b + 1) * RANK] = wide[
                b * slots : (b + 1) * slots, :
            ]
    out[:count, :] = rows[...].astype(BF)
    for k, turned in enumerate((own, first, second, third)):
        for layer in range(3):
            start = count + (k * 3 + layer) * RANK
            for b in range(block // RANK):
                columns = slice(b * RANK, (b + 1) * RANK)
                out[start : start + RANK, columns] = turned[layer, columns, :]


def ready_kernel(partial, base, chosen):
    notes = partial[:, 3 * RANK :]
    place = (notes[:, 6:7] * 8.0 + notes[:, 7:8]).astype(jnp.int32)
    chosen[...] = (place == iota(chosen.shape, 1)).astype(BF)
    base[:, : 3 * RANK] = partial[:, : 3 * RANK].astype(BF)
    rough = notes.astype(BF).astype(F32)
    lane = iota(notes.shape, 1)
    for i in range(3):
        rest = notes[:, i : i + 1] - rough[:, i : i + 1]
        rough = jnp.where(lane == 3 + i, rest, rough)
    base[:, 3 * RANK :] = rough.astype(BF)


def pick_kernel(received, base, chosen, out):
    peers = received.shape[0]
    tail = received[:, received.shape[1] - 8 :, :].astype(F32).reshape(peers * 8, RANK).astype(BF)
    out[:, : 3 * RANK] = base[:, : 3 * RANK]
    out[:, 3 * RANK : 4 * RANK] = dot(chosen[...], tail).astype(BF)
    out[:, 4 * RANK :] = base[:, 3 * RANK :]


def merge_kernel(parts, *refs):
    out = refs[-1]
    total = parts[0].astype(F32)
    for peer in range(1, parts.shape[0]):
        total = total + parts[peer].astype(F32)
    squares = total[:, 4 * RANK :]
    inverse = [
        lax.rsqrt((squares[:, i : i + 1] + squares[:, 3 + i : 4 + i]) / MODEL_WIDTH + EPSILON)
        for i in range(3)
    ]
    mixed = inverse[0] * total[:, :RANK]
    for i in (1, 2):
        mixed = mixed + inverse[i] * total[:, i * RANK : (i + 1) * RANK]
    back = total[:, 3 * RANK : 4 * RANK]
    gate = 1.0 / (1.0 + jnp.exp(-mixed))
    grad = (back * gate * (1.0 + mixed * (1.0 - gate))).astype(BF)
    active = (mixed * gate).astype(BF)
    notes = squares / parts.shape[0]
    lane = iota(notes.shape, 1)
    for i in range(3):
        rough = inverse[i].astype(BF).astype(F32)
        notes = jnp.where(lane == i, rough, notes)
        notes = jnp.where(lane == 3 + i, inverse[i] - rough, notes)
    notes = notes.astype(BF)
    for peer in range(out.shape[0]):
        out[peer, :, :RANK] = grad
        out[peer, :, RANK : 2 * RANK] = active
        out[peer, :, 2 * RANK :] = notes


def grads_kernel(place, slots, merged, out):
    blocks = slots.shape[1] // RANK
    count = slots.shape[0] - NX * 3 * RANK
    peer_slots = NX * MOST
    down = [None] * 3
    placed = None
    for k in range(NX):
        source = (place[0] + NX - k) % NX
        rows = merged[source]
        notes = rows[:, 2 * RANK :].astype(F32)
        grad = rows[:, :RANK].astype(F32)
        for i in range(3):
            inverse = notes[:, i : i + 1] + notes[:, 3 + i : 4 + i]
            start = count + (k * 3 + i) * RANK
            turned = jnp.concatenate(
                [
                    slots[start : start + RANK, b * RANK : (b + 1) * RANK]
                    for b in range(blocks)
                ],
                axis=0,
            )
            term = dot(turned, (inverse * grad).astype(BF))
            down[i] = term if down[i] is None else down[i] + term
        slot = notes[:, 6:7].astype(jnp.int32) * peer_slots + notes[:, 7:8].astype(jnp.int32)
        slot = slot + source * MOST
        chosen = (slot == iota((rows.shape[0], count), 1)).astype(BF)
        term = dot_tn(rows[:, RANK : 2 * RANK], chosen)
        placed = term if placed is None else placed + term
    for i in range(3):
        out[:, i * RANK : (i + 1) * RANK] = down[i].astype(BF)
    up = dot(placed.astype(BF), slots[:count, :]).astype(BF)
    for b in range(blocks):
        out[b * RANK : (b + 1) * RANK, 3 * RANK :] = up[:, b * RANK : (b + 1) * RANK]


def sum_kernel(parts, out):
    total = parts[0].astype(F32)
    for peer in range(1, parts.shape[0]):
        total = total + parts[peer].astype(F32)
    out[...] = jnp.broadcast_to(total.astype(BF)[None], out.shape)


def final_kernel(parts, down, up):
    step = pl.program_id(0)
    z, x = step % parts.shape[0], step // parts.shape[0]
    for b in range(up.shape[1] // RANK):
        rows = slice(b * RANK, (b + 1) * RANK)
        down[rows, :] = parts[z, b, x, :, : 3 * RANK].astype(F32)
        up[:, rows] = parts[z, b, x, :, 3 * RANK :].astype(F32)


def whole(shape):
    return pl.BlockSpec(shape, lambda *_: (0,) * len(shape))


def shape(dims, kind=BF):
    return jax.ShapeDtypeStruct(dims, kind)


def call(kernel, name, out_shape, *args, unread=(), scratch=(), grid=(), limit=32):
    smem = pl.BlockSpec(memory_space=pltpu.SMEM)
    specs = [smem if a.ndim == 1 else whole(a.shape) for a in args]
    specs = specs + [pl.BlockSpec(memory_space=pl.ANY) for _ in unread]
    outs = out_shape if isinstance(out_shape, list) else [out_shape]
    outs = [whole(o.shape) for o in outs]
    return pl.pallas_call(
        kernel,
        grid=grid,
        in_specs=specs,
        out_specs=outs if isinstance(out_shape, list) else outs[0],
        out_shape=out_shape,
        scratch_shapes=[pltpu.VMEM(*s) for s in scratch],
        compiler_params=params(limit),
        cost_estimate=pl.CostEstimate(
            flops=1_000_000, bytes_accessed=2_000_000, transcendentals=0
        ),
        name=name,
    )(*args, *unread)


def body(
    queries,
    tree_keys,
    tree_values,
    cache_keys,
    cache_values,
    parents,
    cache_lengths,
    accepted_counts,
    dest_map,
    low_hidden,
    mid_hidden,
    norm_gains,
    merge_down,
    merge_up,
    out_grad,
):
    count, width = low_hidden.shape
    branches = parents.shape[0]
    nyh, nyl, nzl = lax.axis_size("yh"), lax.axis_size("yl"), lax.axis_size("zl")
    nzh, nc = lax.axis_size("zh"), lax.axis_size("c")
    peers = nyh * nyl * nzl * NX
    block = width // NX
    place = lax.axis_index("x").astype(jnp.int32).reshape(1)
    smem = pl.BlockSpec(memory_space=pltpu.SMEM)
    together = 2
    row_block = pl.BlockSpec((together * TREE, width), lambda b: (b, 0))
    cache_block = pl.BlockSpec((together, CACHE, HEAD_DIM), lambda b: (b, 0, 0))

    height = block // RANK * NX * MOST + 8
    packed = call(
        pack_kernel,
        "pack",
        shape((peers, height, RANK)),
        out_grad,
        merge_up,
        scratch=[((peers, height, RANK), F32)],
        grid=(1,),
        limit=60,
    )
    received = lax.all_to_all(packed, ("yh", "yl", "zl", "x"), 0, 0, tiled=True)
    *turned, partial = pl.pallas_call(
        feature_kernel,
        grid=(branches // together,),
        in_specs=[
            smem,
            smem,
            smem,
            whole((count, 1)),
            whole((branches, TREE)),
            row_block,
            whole((count, HEAD_DIM)),
            whole((count, HEAD_DIM)),
            cache_block,
            cache_block,
            row_block,
            row_block,
            whole((3, width)),
            whole((width, 3 * RANK)),
        ],
        out_specs=[pl.BlockSpec(memory_space=pltpu.HBM)] * NX + [whole((count, 4 * RANK))],
        out_shape=[shape((3, block, count))] * NX + [shape((count, 4 * RANK), F32)],
        scratch_shapes=[
            pltpu.VMEM((count, count), F32),
            pltpu.VMEM((3, count, width), BF),
            pltpu.VMEM((count, RANK), F32),
            pltpu.VMEM((NX, 3, block, count), BF),
            pltpu.SemaphoreType.DMA((NX,)),
        ],
        compiler_params=params(60),
        cost_estimate=pl.CostEstimate(
            flops=400_000_000, bytes_accessed=8_000_000, transcendentals=600_000
        ),
        name="features",
    )(
        place,
        cache_lengths,
        accepted_counts,
        dest_map,
        parents,
        queries,
        tree_keys,
        tree_values,
        cache_keys,
        cache_values,
        low_hidden,
        mid_hidden,
        norm_gains,
        merge_down,
    )
    for k in range(1, NX):
        turned[k] = lax.ppermute(turned[k], "x", [(i, (i + k) % NX) for i in range(NX)])
    base, chosen = call(
        ready_kernel, "ready", [shape((count, 4 * RANK)), shape((count, peers * 8))], partial
    )
    sent = call(pick_kernel, "pick", shape((count, 5 * RANK)), received, base, chosen)
    share = count // (nzh * nc)
    parts = lax.all_to_all(sent.reshape(nzh * nc, share, 5 * RANK), ("zh", "c"), 0, 0, tiled=True)
    merged = call(
        merge_kernel,
        "merge",
        shape((NX * nzh * nc, share, 3 * RANK)),
        parts,
        unread=turned[1:],
    )
    merged = lax.all_to_all(merged, ("x", "zh", "c"), 0, 0, tiled=True)
    merged = merged.reshape(NX, count, 3 * RANK)
    slots = call(
        unpack_kernel,
        "unpack",
        shape((peers * NX * MOST + NX * 3 * RANK, block)),
        received,
        *turned,
        scratch=[((peers * NX * MOST, block), F32)],
    )
    grads = call(grads_kernel, "grads", shape((block, 4 * RANK)), place, slots, merged)
    piece = block // (nzl * nyl * nyh)
    grads = lax.all_to_all(
        grads.reshape(nzl * nyl * nyh, piece, 4 * RANK), ("zl", "yl", "yh"), 0, 0, tiled=True
    )
    grads = call(sum_kernel, "total", shape((nyh, piece, 4 * RANK)), grads)
    rows = nyh * piece
    grads = lax.all_to_all(grads, "yh", 0, 0, tiled=True).reshape(rows, 4 * RANK)
    near = nzl * nyl
    grads = jnp.broadcast_to(grads[None], (near * NX, rows, 4 * RANK))
    grads = lax.all_to_all(grads, ("zl", "yl", "x"), 0, 0, tiled=True)
    grads = grads.reshape(nzl, nyl, NX, rows, 4 * RANK)
    step = nyl * rows
    return pl.pallas_call(
        final_kernel,
        grid=(nzl * NX,),
        in_specs=[pl.BlockSpec(memory_space=pltpu.VMEM)],
        out_specs=[
            pl.BlockSpec((step, 3 * RANK), lambda i: (i, 0)),
            pl.BlockSpec((RANK, step), lambda i: (0, i)),
        ],
        out_shape=[shape((width, 3 * RANK), F32), shape((RANK, width), F32)],
        compiler_params=params(),
        name="final",
    )(grads)


def solution(mesh):
    fine = Mesh(mesh.devices.reshape(4, 2, 2, NX, 4, 2), ("yh", "yl", "zl", "x", "zh", "c"))
    dp, head = ("yh", "yl", "zl", "x"), ("zh", "c")
    placed = (
        P(dp, head),
        P(dp, head),
        P(dp, head),
        P(dp, None, head),
        P(dp, None, head),
        P(dp, None),
        P(dp),
        P(dp),
        P(dp, None),
        P(dp, head),
        P(dp, head),
        P(None, head),
        P(head, None),
        P(None, head),
        P(dp, head),
    )
    return jax.shard_map(
        body,
        mesh=fine,
        in_specs=placed,
        out_specs=(P(head, None), P(None, head)),
        check_vma=False,
    )
```

```python
import jax
import jax.numpy as jnp
from jax import lax
from jax.experimental import pallas as pl
from jax.experimental.pallas import tpu as pltpu
from jax.sharding import Mesh, PartitionSpec as P

MODEL_WIDTH = 16384
HEAD_DIM = 128
TREE = 16
CACHE = 128
RANK = 128
MOST = 3
NX = 4
PEERS = 64
EPSILON = 1e-05
MASKED = -1e30
BF = jnp.bfloat16
F32 = jnp.float32
MIB = 1024 * 1024


def params(limit=32):
    return pltpu.CompilerParams(vmem_limit_bytes=limit * MIB)


def iota(shape, dim):
    return lax.broadcasted_iota(jnp.int32, shape, dim)


def dot(a, b):
    return jnp.dot(a, b, preferred_element_type=F32)


def dot_nt(a, b):
    return lax.dot_general(a, b, (((1,), (1,)), ((), ())), preferred_element_type=F32)


def dot_tn(a, b):
    return lax.dot_general(a, b, (((0,), (0,)), ((), ())), preferred_element_type=F32)


def feature_kernel(
    place,
    lengths,
    counts,
    targets,
    parents,
    queries,
    tree_keys,
    tree_values,
    cache_keys,
    cache_values,
    low,
    mid,
    gains,
    merge_down,
    own,
    first,
    second,
    third,
    partial,
    reach,
    rows,
    squares,
    turned,
    sent,
):
    together = cache_keys.shape[0]
    count, width = rows.shape[1], rows.shape[2]
    heads = width // HEAD_DIM

    @pl.when(pl.program_id(0) == 0)
    def _():
        groups = parents.shape[0]
        owner = (iota((count, groups), 0) // TREE == iota((count, groups), 1)).astype(F32)
        spread = jnp.dot(owner, parents[...].astype(F32), preferred_element_type=F32)
        same = iota((count, TREE), 0) % TREE == iota((count, TREE), 1)
        parent = jnp.sum(jnp.where(same, spread, 0.0), axis=1, keepdims=True).astype(jnp.int32)
        row, column = iota((count, count), 0), iota((count, count), 1)
        linked = (column == row) | ((parent >= 0) & (column == row // TREE * TREE + parent))
        reached = jnp.where(linked, 1.0, 0.0)
        for _ in range((TREE - 1).bit_length()):
            step = reached.astype(BF)
            reached = jnp.minimum(dot(step, step), 1.0)
        reach[...] = reached

    for j in range(together):
        branch = pl.program_id(0) * together + j
        start = pl.multiple_of(branch * TREE, TREE)
        mine = slice(j * TREE, (j + 1) * TREE)
        here = pl.ds(start, TREE)
        query = queries[mine, :]
        query = jnp.concatenate(
            [query[:, h * HEAD_DIM : (h + 1) * HEAD_DIM] for h in range(heads)], axis=0
        )
        keys = jnp.concatenate([cache_keys[j], tree_keys[...]], axis=0)
        values = jnp.concatenate([cache_values[j], tree_values[...]], axis=0)
        scores = dot_nt(query, keys) * (HEAD_DIM**-0.5)
        live = jnp.where(iota((TREE, CACHE), 1) < lengths[branch], 1.0, 0.0)
        seen = jnp.concatenate([live, reach[here, :]], axis=1) > 0.5
        scores = jnp.where(seen[None], scores.reshape(heads, TREE, CACHE + count), MASKED)
        weights = jnp.exp(scores - jnp.max(scores, axis=2, keepdims=True))
        probs = (weights / jnp.sum(weights, axis=2, keepdims=True)).astype(BF)
        attended = dot(probs.reshape(heads * TREE, CACHE + count), values).astype(BF)
        attended = jnp.concatenate(
            [attended[h * TREE : (h + 1) * TREE, :] for h in range(heads)], axis=1
        )
        kept = iota((TREE, 1), 0) < counts[branch]
        lane = iota((TREE, RANK), 1)
        totals = jnp.zeros((TREE, RANK), F32)
        for layer, feature in enumerate((low[mine, :], mid[mine, :], attended)):
            feature = jnp.where(kept, feature.astype(F32), 0.0)
            total = jnp.sum(feature * feature, axis=1, keepdims=True)
            totals = totals + jnp.where(lane == layer, total, 0.0)
            gain = gains[layer : layer + 1, :].astype(F32)
            rows[layer, here, :] = (feature * gain).astype(BF)
        squares[here, :] = totals

    @pl.when(pl.program_id(0) == pl.num_programs(0) - 1)
    def _():
        block = own.shape[1]
        copies = []
        for k, out in enumerate((own, first, second, third)):
            chunk = (place[0] + k) % (width // block)
            chunk = pl.ds(pl.multiple_of(chunk * block, block), block)
            for layer in range(3):
                turned[k, layer] = rows[layer, :, chunk].T
            copies.append(pltpu.make_async_copy(turned.at[k], out, sent.at[k]))
            copies[k].start()
        for layer in range(3):
            columns = slice(layer * RANK, (layer + 1) * RANK)
            partial[:, columns] = dot(rows[layer], merge_down[:, columns])
        target = targets[...]
        named = (target == iota((count, PEERS), 1)).astype(F32)
        earlier = (iota((count, count), 0) > iota((count, count), 1)).astype(BF)
        rank = jnp.sum(dot(earlier, named.astype(BF)) * named, axis=1, keepdims=True)
        notes = squares[...]
        lane = iota((count, RANK), 1)
        for i, note in ((6, target.astype(F32)), (7, rank)):
            notes = jnp.where(lane == i, note, notes)
        partial[:, 3 * RANK :] = notes
        for copy in copies:
            copy.wait()


def pack_kernel(grads, merge_up, out, rows):
    peers, height = out.shape[0], out.shape[1]
    slots = grads.shape[0] // (peers // NX)
    blocks = grads.shape[1] // NX // RANK
    wide = grads[...].astype(F32)
    products = dot_nt(grads[...], merge_up[...])
    rows[:, blocks * slots :, :] = jnp.zeros((peers, height - blocks * slots, RANK), F32)
    for x in range(NX):
        for b in range(blocks):
            column = (x * blocks + b) * RANK
            for g in range(peers // NX):
                rows[g * NX + x, b * slots : (b + 1) * slots, :] = wide[
                    g * slots : (g + 1) * slots, column : column + RANK
                ]
    for d in range(peers):
        rows[d, blocks * slots : blocks * slots + MOST, :] = products[d * MOST : (d + 1) * MOST, :]
    out[...] = rows[...].astype(BF)


def unpack_kernel(received, own, first, second, third, out, rows):
    peers = received.shape[0]
    count, block = rows.shape[0], own.shape[1]
    slots = count // peers
    for b in range(block // RANK):
        for j in range(peers):
            rows[j * slots : (j + 1) * slots, :] = received[j].astype(F32)[
                b * slots : (b + 1) * slots, :
            ]
        out[b * count : (b + 1) * count, :] = rows[...].astype(BF)
    start = count * (block // RANK)
    for turned in (own, first, second, third):
        for layer in range(3):
            out[start : start + block, :] = turned[layer]
            start = start + block


def ready_kernel(partial, base, chosen):
    notes = partial[:, 3 * RANK :]
    place = (notes[:, 6:7] * 8.0 + notes[:, 7:8]).astype(jnp.int32)
    chosen[...] = (place == iota(chosen.shape, 1)).astype(BF)
    base[:, : 3 * RANK] = partial[:, : 3 * RANK].astype(BF)
    rough = notes.astype(BF).astype(F32)
    lane = iota(notes.shape, 1)
    for i in range(3):
        rest = notes[:, i : i + 1] - rough[:, i : i + 1]
        rough = jnp.where(lane == 3 + i, rest, rough)
    base[:, 3 * RANK :] = rough.astype(BF)


def pick_kernel(received, base, chosen, out):
    peers = received.shape[0]
    tail = received[:, received.shape[1] - 8 :, :].astype(F32).reshape(peers * 8, RANK).astype(BF)
    out[:, : 3 * RANK] = base[:, : 3 * RANK]
    out[:, 3 * RANK : 4 * RANK] = dot(chosen[...], tail).astype(BF)
    out[:, 4 * RANK :] = base[:, 3 * RANK :]


def merge_kernel(parts, *refs):
    out = refs[-1]
    total = parts[0].astype(F32)
    for peer in range(1, parts.shape[0]):
        total = total + parts[peer].astype(F32)
    squares = total[:, 4 * RANK :]
    inverse = [
        lax.rsqrt((squares[:, i : i + 1] + squares[:, 3 + i : 4 + i]) / MODEL_WIDTH + EPSILON)
        for i in range(3)
    ]
    mixed = inverse[0] * total[:, :RANK]
    for i in (1, 2):
        mixed = mixed + inverse[i] * total[:, i * RANK : (i + 1) * RANK]
    back = total[:, 3 * RANK : 4 * RANK]
    gate = 1.0 / (1.0 + jnp.exp(-mixed))
    grad = (back * gate * (1.0 + mixed * (1.0 - gate))).astype(BF)
    active = (mixed * gate).astype(BF)
    notes = squares / parts.shape[0]
    lane = iota(notes.shape, 1)
    for i in range(3):
        rough = inverse[i].astype(BF).astype(F32)
        notes = jnp.where(lane == i, rough, notes)
        notes = jnp.where(lane == 3 + i, inverse[i] - rough, notes)
    notes = notes.astype(BF)
    for peer in range(out.shape[0]):
        out[peer, :, :RANK] = grad
        out[peer, :, RANK : 2 * RANK] = active
        out[peer, :, 2 * RANK :] = notes


def grads_kernel(place, slots, merged, out):
    block = out.shape[0]
    blocks = block // RANK
    count = slots.shape[0] // blocks - NX * 3 * RANK
    peer_slots = NX * MOST
    down = [None] * 3
    placed = None
    for k in range(NX):
        source = (place[0] + NX - k) % NX
        rows = merged[source]
        notes = rows[:, 2 * RANK :].astype(F32)
        grad = rows[:, :RANK].astype(F32)
        for i in range(3):
            inverse = notes[:, i : i + 1] + notes[:, 3 + i : 4 + i]
            start = count * blocks + (k * 3 + i) * block
            turned = slots[start : start + block, :]
            term = dot(turned, (inverse * grad).astype(BF))
            down[i] = term if down[i] is None else down[i] + term
        slot = notes[:, 6:7].astype(jnp.int32) * peer_slots + notes[:, 7:8].astype(jnp.int32)
        slot = slot + source * MOST
        chosen = (slot == iota((rows.shape[0], count), 1)).astype(BF)
        term = dot_tn(rows[:, RANK : 2 * RANK], chosen)
        placed = term if placed is None else placed + term
    for i in range(3):
        out[:, i * RANK : (i + 1) * RANK] = down[i].astype(BF)
    placed = placed.astype(BF)
    for b in range(blocks):
        up = dot(placed, slots[b * count : (b + 1) * count, :])
        out[b * RANK : (b + 1) * RANK, 3 * RANK :] = up.astype(BF)


def sum_kernel(parts, out):
    total = parts[0].astype(F32)
    for peer in range(1, parts.shape[0]):
        total = total + parts[peer].astype(F32)
    out[...] = jnp.broadcast_to(total.astype(BF)[None], out.shape)


def final_kernel(parts, down_out, up_out, down, up, sems):
    near, rows = parts.shape[0] * parts.shape[1], parts.shape[3]
    copies = []
    for x in range(parts.shape[2]):
        for n in range(near):
            z, y = n // parts.shape[1], n % parts.shape[1]
            piece = pl.ds((x * near + n) * rows, rows)
            down[piece, :] = parts[z, y, x, :, : 3 * RANK].astype(F32)
            up[:, piece] = parts[z, y, x, :, 3 * RANK :].astype(F32)
        mine = pl.ds(x * near * rows, near * rows)
        copies.append(pltpu.make_async_copy(down.at[mine], down_out.at[mine], sems.at[0, x]))
        copies.append(pltpu.make_async_copy(up.at[:, mine], up_out.at[:, mine], sems.at[1, x]))
        for copy in copies[-2:]:
            copy.start()
    for copy in copies:
        copy.wait()


def whole(shape):
    return pl.BlockSpec(shape, lambda *_: (0,) * len(shape))


def shape(dims, kind=BF):
    return jax.ShapeDtypeStruct(dims, kind)


def call(kernel, name, out_shape, *args, unread=(), scratch=(), grid=(), limit=32):
    smem = pl.BlockSpec(memory_space=pltpu.SMEM)
    specs = [smem if a.ndim == 1 else whole(a.shape) for a in args]
    specs = specs + [pl.BlockSpec(memory_space=pl.ANY) for _ in unread]
    outs = out_shape if isinstance(out_shape, list) else [out_shape]
    outs = [whole(o.shape) for o in outs]
    return pl.pallas_call(
        kernel,
        grid=grid,
        in_specs=specs,
        out_specs=outs if isinstance(out_shape, list) else outs[0],
        out_shape=out_shape,
        scratch_shapes=[pltpu.VMEM(*s) for s in scratch],
        compiler_params=params(limit),
        cost_estimate=pl.CostEstimate(
            flops=1_000_000, bytes_accessed=2_000_000, transcendentals=0
        ),
        name=name,
    )(*args, *unread)


def body(
    queries,
    tree_keys,
    tree_values,
    cache_keys,
    cache_values,
    parents,
    cache_lengths,
    accepted_counts,
    dest_map,
    low_hidden,
    mid_hidden,
    norm_gains,
    merge_down,
    merge_up,
    out_grad,
):
    count, width = low_hidden.shape
    branches = parents.shape[0]
    nyh, nyl, nzl = lax.axis_size("yh"), lax.axis_size("yl"), lax.axis_size("zl")
    nzh, nc = lax.axis_size("zh"), lax.axis_size("c")
    peers = nyh * nyl * nzl * NX
    block = width // NX
    place = lax.axis_index("x").astype(jnp.int32).reshape(1)
    smem = pl.BlockSpec(memory_space=pltpu.SMEM)
    together = 2
    row_block = pl.BlockSpec((together * TREE, width), lambda b: (b, 0))
    cache_block = pl.BlockSpec((together, CACHE, HEAD_DIM), lambda b: (b, 0, 0))

    height = block // RANK * NX * MOST + 8
    packed = call(
        pack_kernel,
        "pack",
        shape((peers, height, RANK)),
        out_grad,
        merge_up,
        scratch=[((peers, height, RANK), F32)],
        grid=(1,),
        limit=60,
    )
    received = lax.all_to_all(packed, ("yh", "yl", "zl", "x"), 0, 0, tiled=True)
    *turned, partial = pl.pallas_call(
        feature_kernel,
        grid=(branches // together,),
        in_specs=[
            smem,
            smem,
            smem,
            whole((count, 1)),
            whole((branches, TREE)),
            row_block,
            whole((count, HEAD_DIM)),
            whole((count, HEAD_DIM)),
            cache_block,
            cache_block,
            row_block,
            row_block,
            whole((3, width)),
            whole((width, 3 * RANK)),
        ],
        out_specs=[pl.BlockSpec(memory_space=pltpu.HBM)] * NX + [whole((count, 4 * RANK))],
        out_shape=[shape((3, block, count))] * NX + [shape((count, 4 * RANK), F32)],
        scratch_shapes=[
            pltpu.VMEM((count, count), F32),
            pltpu.VMEM((3, count, width), BF),
            pltpu.VMEM((count, RANK), F32),
            pltpu.VMEM((NX, 3, block, count), BF),
            pltpu.SemaphoreType.DMA((NX,)),
        ],
        compiler_params=params(60),
        cost_estimate=pl.CostEstimate(
            flops=400_000_000, bytes_accessed=8_000_000, transcendentals=600_000
        ),
        name="features",
    )(
        place,
        cache_lengths,
        accepted_counts,
        dest_map,
        parents,
        queries,
        tree_keys,
        tree_values,
        cache_keys,
        cache_values,
        low_hidden,
        mid_hidden,
        norm_gains,
        merge_down,
    )
    for k in range(1, NX):
        turned[k] = lax.ppermute(turned[k], "x", [(i, (i + k) % NX) for i in range(NX)])
    base, chosen = call(
        ready_kernel, "ready", [shape((count, 4 * RANK)), shape((count, peers * 8))], partial
    )
    sent = call(pick_kernel, "pick", shape((count, 5 * RANK)), received, base, chosen)
    share = count // (nzh * nc)
    parts = lax.all_to_all(sent.reshape(nzh * nc, share, 5 * RANK), ("zh", "c"), 0, 0, tiled=True)
    merged = call(
        merge_kernel,
        "merge",
        shape((NX * nzh * nc, share, 3 * RANK)),
        parts,
        unread=turned[1:],
    )
    merged = lax.all_to_all(merged, ("x", "zh", "c"), 0, 0, tiled=True)
    merged = merged.reshape(NX, count, 3 * RANK)
    slots = call(
        unpack_kernel,
        "unpack",
        shape((block // RANK * peers * NX * MOST + NX * 3 * block, RANK)),
        received,
        *turned,
        scratch=[((peers * NX * MOST, RANK), F32)],
    )
    grads = call(grads_kernel, "grads", shape((block, 4 * RANK)), place, slots, merged)
    piece = block // (nzl * nyl * nyh)
    grads = lax.all_to_all(
        grads.reshape(nzl * nyl * nyh, piece, 4 * RANK), ("zl", "yl", "yh"), 0, 0, tiled=True
    )
    grads = call(sum_kernel, "total", shape((nyh, piece, 4 * RANK)), grads)
    rows = nyh * piece
    grads = lax.all_to_all(grads, "yh", 0, 0, tiled=True).reshape(rows, 4 * RANK)
    near = nzl * nyl
    grads = jnp.broadcast_to(grads[None], (near * NX, rows, 4 * RANK))
    grads = lax.all_to_all(grads, ("zl", "yl", "x"), 0, 0, tiled=True)
    grads = grads.reshape(nzl, nyl, NX, rows, 4 * RANK)
    return pl.pallas_call(
        final_kernel,
        in_specs=[pl.BlockSpec(memory_space=pltpu.VMEM)],
        out_specs=[pl.BlockSpec(memory_space=pl.ANY)] * 2,
        out_shape=[shape((width, 3 * RANK), F32), shape((RANK, width), F32)],
        scratch_shapes=[
            pltpu.VMEM((width, 3 * RANK), F32),
            pltpu.VMEM((RANK, width), F32),
            pltpu.SemaphoreType.DMA((2, NX)),
        ],
        compiler_params=params(),
        name="final",
    )(grads)


def solution(mesh):
    fine = Mesh(mesh.devices.reshape(4, 2, 2, NX, 4, 2), ("yh", "yl", "zl", "x", "zh", "c"))
    dp, head = ("yh", "yl", "zl", "x"), ("zh", "c")
    placed = (
        P(dp, head),
        P(dp, head),
        P(dp, head),
        P(dp, None, head),
        P(dp, None, head),
        P(dp, None),
        P(dp),
        P(dp),
        P(dp, None),
        P(dp, head),
        P(dp, head),
        P(None, head),
        P(head, None),
        P(None, head),
        P(dp, head),
    )
    return jax.shard_map(
        body,
        mesh=fine,
        in_specs=placed,
        out_specs=(P(head, None), P(None, head)),
        check_vma=False,
    )
```

```python
import jax
import jax.numpy as jnp
from jax import lax
from jax.experimental import pallas as pl
from jax.experimental.pallas import tpu as pltpu
from jax.sharding import Mesh, PartitionSpec as P

MODEL_WIDTH = 16384
HEAD_DIM = 128
TREE = 16
CACHE = 128
RANK = 128
MOST = 3
NX = 4
PEERS = 64
SHIFTS = (0, 2, 1, 3)
EPSILON = 1e-05
MASKED = -1e30
BF = jnp.bfloat16
F32 = jnp.float32
MIB = 1024 * 1024


def params(limit=32):
    return pltpu.CompilerParams(vmem_limit_bytes=limit * MIB)


def iota(shape, dim):
    return lax.broadcasted_iota(jnp.int32, shape, dim)


def dot(a, b):
    return jnp.dot(a, b, preferred_element_type=F32)


def dot_nt(a, b):
    return lax.dot_general(a, b, (((1,), (1,)), ((), ())), preferred_element_type=F32)


def dot_tn(a, b):
    return lax.dot_general(a, b, (((0,), (0,)), ((), ())), preferred_element_type=F32)


def feature_kernel(
    place,
    lengths,
    counts,
    targets,
    parents,
    queries,
    tree_keys,
    tree_values,
    cache_keys,
    cache_values,
    low,
    mid,
    gains,
    merge_down,
    own,
    first,
    second,
    third,
    partial,
    reach,
    rows,
    squares,
    turned,
    sent,
):
    together = cache_keys.shape[0]
    count, width = rows.shape[1], rows.shape[2]
    heads = width // HEAD_DIM

    @pl.when(pl.program_id(0) == 0)
    def _():
        groups = parents.shape[0]
        owner = (iota((count, groups), 0) // TREE == iota((count, groups), 1)).astype(F32)
        spread = jnp.dot(owner, parents[...].astype(F32), preferred_element_type=F32)
        same = iota((count, TREE), 0) % TREE == iota((count, TREE), 1)
        parent = jnp.sum(jnp.where(same, spread, 0.0), axis=1, keepdims=True).astype(jnp.int32)
        row, column = iota((count, count), 0), iota((count, count), 1)
        linked = (column == row) | ((parent >= 0) & (column == row // TREE * TREE + parent))
        reached = jnp.where(linked, 1.0, 0.0)
        for _ in range((TREE - 1).bit_length()):
            step = reached.astype(BF)
            reached = jnp.minimum(dot(step, step), 1.0)
        reach[...] = reached

    for j in range(together):
        branch = pl.program_id(0) * together + j
        start = pl.multiple_of(branch * TREE, TREE)
        mine = slice(j * TREE, (j + 1) * TREE)
        here = pl.ds(start, TREE)
        query = queries[mine, :]
        query = jnp.concatenate(
            [query[:, h * HEAD_DIM : (h + 1) * HEAD_DIM] for h in range(heads)], axis=0
        )
        keys = jnp.concatenate([cache_keys[j], tree_keys[...]], axis=0)
        values = jnp.concatenate([cache_values[j], tree_values[...]], axis=0)
        scores = dot_nt(query, keys) * (HEAD_DIM**-0.5)
        live = jnp.where(iota((TREE, CACHE), 1) < lengths[branch], 1.0, 0.0)
        seen = jnp.concatenate([live, reach[here, :]], axis=1) > 0.5
        scores = jnp.where(seen[None], scores.reshape(heads, TREE, CACHE + count), MASKED)
        weights = jnp.exp(scores - jnp.max(scores, axis=2, keepdims=True))
        probs = (weights / jnp.sum(weights, axis=2, keepdims=True)).astype(BF)
        attended = dot(probs.reshape(heads * TREE, CACHE + count), values).astype(BF)
        attended = jnp.concatenate(
            [attended[h * TREE : (h + 1) * TREE, :] for h in range(heads)], axis=1
        )
        kept = iota((TREE, 1), 0) < counts[branch]
        lane = iota((TREE, RANK), 1)
        totals = jnp.zeros((TREE, RANK), F32)
        for layer, feature in enumerate((low[mine, :], mid[mine, :], attended)):
            feature = jnp.where(kept, feature.astype(F32), 0.0)
            total = jnp.sum(feature * feature, axis=1, keepdims=True)
            totals = totals + jnp.where(lane == layer, total, 0.0)
            gain = gains[layer : layer + 1, :].astype(F32)
            rows[layer, here, :] = (feature * gain).astype(BF)
        squares[here, :] = totals

    @pl.when(pl.program_id(0) == pl.num_programs(0) - 1)
    def _():
        block = own.shape[1]
        copies = []
        for k, out in enumerate((own, first, second, third)):
            chunk = (place[0] + SHIFTS[k]) % (width // block)
            chunk = pl.ds(pl.multiple_of(chunk * block, block), block)
            for layer in range(3):
                turned[k, layer] = rows[layer, :, chunk].T
            copies.append(pltpu.make_async_copy(turned.at[k], out, sent.at[k]))
            copies[k].start()
        for layer in range(3):
            columns = slice(layer * RANK, (layer + 1) * RANK)
            partial[:, columns] = dot(rows[layer], merge_down[:, columns])
        target = targets[...]
        named = (target == iota((count, PEERS), 1)).astype(F32)
        earlier = (iota((count, count), 0) > iota((count, count), 1)).astype(BF)
        rank = jnp.sum(dot(earlier, named.astype(BF)) * named, axis=1, keepdims=True)
        notes = squares[...]
        lane = iota((count, RANK), 1)
        for i, note in ((6, target.astype(F32)), (7, rank)):
            notes = jnp.where(lane == i, note, notes)
        partial[:, 3 * RANK :] = notes
        for copy in copies:
            copy.wait()


def pack_kernel(grads, merge_up, out, rows):
    peers, height = out.shape[0], out.shape[1]
    slots = grads.shape[0] // (peers // NX)
    blocks = grads.shape[1] // NX // RANK
    wide = grads[...].astype(F32)
    products = dot_nt(grads[...], merge_up[...])
    rows[:, blocks * slots :, :] = jnp.zeros((peers, height - blocks * slots, RANK), F32)
    for x in range(NX):
        for b in range(blocks):
            column = (x * blocks + b) * RANK
            for g in range(peers // NX):
                rows[g * NX + x, b * slots : (b + 1) * slots, :] = wide[
                    g * slots : (g + 1) * slots, column : column + RANK
                ]
    for d in range(peers):
        rows[d, blocks * slots : blocks * slots + MOST, :] = products[d * MOST : (d + 1) * MOST, :]
    out[...] = rows[...].astype(BF)


def unpack_kernel(received, own, first, second, third, out, rows):
    peers = received.shape[0]
    count, block = rows.shape[0], own.shape[1]
    slots = count // peers
    for b in range(block // RANK):
        for j in range(peers):
            rows[j * slots : (j + 1) * slots, :] = received[j].astype(F32)[
                b * slots : (b + 1) * slots, :
            ]
        out[b * count : (b + 1) * count, :] = rows[...].astype(BF)
    start = count * (block // RANK)
    for turned in (own, first, second, third):
        for layer in range(3):
            out[start : start + block, :] = turned[layer]
            start = start + block


def ready_kernel(partial, base, chosen):
    notes = partial[:, 3 * RANK :]
    place = (notes[:, 6:7] * 8.0 + notes[:, 7:8]).astype(jnp.int32)
    chosen[...] = (place == iota(chosen.shape, 1)).astype(BF)
    base[:, : 3 * RANK] = partial[:, : 3 * RANK].astype(BF)
    rough = notes.astype(BF).astype(F32)
    lane = iota(notes.shape, 1)
    for i in range(3):
        rest = notes[:, i : i + 1] - rough[:, i : i + 1]
        rough = jnp.where(lane == 3 + i, rest, rough)
    base[:, 3 * RANK :] = rough.astype(BF)


def pick_kernel(received, base, chosen, out):
    peers = received.shape[0]
    tail = received[:, received.shape[1] - 8 :, :].astype(F32).reshape(peers * 8, RANK).astype(BF)
    out[:, : 3 * RANK] = base[:, : 3 * RANK]
    out[:, 3 * RANK : 4 * RANK] = dot(chosen[...], tail).astype(BF)
    out[:, 4 * RANK :] = base[:, 3 * RANK :]


def merge_kernel(parts, *refs):
    out = refs[-1]
    total = parts[0].astype(F32)
    for peer in range(1, parts.shape[0]):
        total = total + parts[peer].astype(F32)
    squares = total[:, 4 * RANK :]
    inverse = [
        lax.rsqrt((squares[:, i : i + 1] + squares[:, 3 + i : 4 + i]) / MODEL_WIDTH + EPSILON)
        for i in range(3)
    ]
    mixed = inverse[0] * total[:, :RANK]
    for i in (1, 2):
        mixed = mixed + inverse[i] * total[:, i * RANK : (i + 1) * RANK]
    back = total[:, 3 * RANK : 4 * RANK]
    gate = 1.0 / (1.0 + jnp.exp(-mixed))
    grad = (back * gate * (1.0 + mixed * (1.0 - gate))).astype(BF)
    active = (mixed * gate).astype(BF)
    notes = squares / parts.shape[0]
    lane = iota(notes.shape, 1)
    for i in range(3):
        rough = inverse[i].astype(BF).astype(F32)
        notes = jnp.where(lane == i, rough, notes)
        notes = jnp.where(lane == 3 + i, inverse[i] - rough, notes)
    notes = notes.astype(BF)
    for peer in range(out.shape[0]):
        out[peer, :, :RANK] = grad
        out[peer, :, RANK : 2 * RANK] = active
        out[peer, :, 2 * RANK :] = notes


def grads_kernel(place, slots, merged, out):
    block = out.shape[0]
    blocks = block // RANK
    count = slots.shape[0] // blocks - NX * 3 * RANK
    peer_slots = NX * MOST
    down = [None] * 3
    placed = None
    for k in range(NX):
        source = (place[0] + NX - SHIFTS[k]) % NX
        rows = merged[source]
        notes = rows[:, 2 * RANK :].astype(F32)
        grad = rows[:, :RANK].astype(F32)
        for i in range(3):
            inverse = notes[:, i : i + 1] + notes[:, 3 + i : 4 + i]
            start = count * blocks + (k * 3 + i) * block
            turned = slots[start : start + block, :]
            term = dot(turned, (inverse * grad).astype(BF))
            down[i] = term if down[i] is None else down[i] + term
        slot = notes[:, 6:7].astype(jnp.int32) * peer_slots + notes[:, 7:8].astype(jnp.int32)
        slot = slot + source * MOST
        chosen = (slot == iota((rows.shape[0], count), 1)).astype(BF)
        term = dot_tn(rows[:, RANK : 2 * RANK], chosen)
        placed = term if placed is None else placed + term
    for i in range(3):
        out[:, i * RANK : (i + 1) * RANK] = down[i].astype(BF)
    placed = placed.astype(BF)
    for b in range(blocks):
        up = dot(placed, slots[b * count : (b + 1) * count, :])
        out[b * RANK : (b + 1) * RANK, 3 * RANK :] = up.astype(BF)


def sum_kernel(parts, out):
    total = parts[0].astype(F32)
    for peer in range(1, parts.shape[0]):
        total = total + parts[peer].astype(F32)
    out[...] = jnp.broadcast_to(total.astype(BF)[None], out.shape)


def final_kernel(parts, down_out, up_out, down, up, sems):
    near, rows = parts.shape[0] * parts.shape[1], parts.shape[3]
    copies = []
    for x in range(parts.shape[2]):
        for n in range(near):
            z, y = n // parts.shape[1], n % parts.shape[1]
            piece = pl.ds((x * near + n) * rows, rows)
            down[piece, :] = parts[z, y, x, :, : 3 * RANK].astype(F32)
            up[:, piece] = parts[z, y, x, :, 3 * RANK :].astype(F32)
        mine = pl.ds(x * near * rows, near * rows)
        copies.append(pltpu.make_async_copy(down.at[mine], down_out.at[mine], sems.at[0, x]))
        copies.append(pltpu.make_async_copy(up.at[:, mine], up_out.at[:, mine], sems.at[1, x]))
        for copy in copies[-2:]:
            copy.start()
    for copy in copies:
        copy.wait()


def whole(shape):
    return pl.BlockSpec(shape, lambda *_: (0,) * len(shape))


def shape(dims, kind=BF):
    return jax.ShapeDtypeStruct(dims, kind)


def call(kernel, name, out_shape, *args, unread=(), scratch=(), grid=(), limit=32):
    smem = pl.BlockSpec(memory_space=pltpu.SMEM)
    specs = [smem if a.ndim == 1 else whole(a.shape) for a in args]
    specs = specs + [pl.BlockSpec(memory_space=pl.ANY) for _ in unread]
    outs = out_shape if isinstance(out_shape, list) else [out_shape]
    outs = [whole(o.shape) for o in outs]
    return pl.pallas_call(
        kernel,
        grid=grid,
        in_specs=specs,
        out_specs=outs if isinstance(out_shape, list) else outs[0],
        out_shape=out_shape,
        scratch_shapes=[pltpu.VMEM(*s) for s in scratch],
        compiler_params=params(limit),
        cost_estimate=pl.CostEstimate(
            flops=1_000_000, bytes_accessed=2_000_000, transcendentals=0
        ),
        name=name,
    )(*args, *unread)


def body(
    queries,
    tree_keys,
    tree_values,
    cache_keys,
    cache_values,
    parents,
    cache_lengths,
    accepted_counts,
    dest_map,
    low_hidden,
    mid_hidden,
    norm_gains,
    merge_down,
    merge_up,
    out_grad,
):
    count, width = low_hidden.shape
    branches = parents.shape[0]
    nyh, nyl, nzl = lax.axis_size("yh"), lax.axis_size("yl"), lax.axis_size("zl")
    nzh, nc = lax.axis_size("zh"), lax.axis_size("c")
    peers = nyh * nyl * nzl * NX
    block = width // NX
    place = lax.axis_index("x").astype(jnp.int32).reshape(1)
    smem = pl.BlockSpec(memory_space=pltpu.SMEM)
    together = 2
    row_block = pl.BlockSpec((together * TREE, width), lambda b: (b, 0))
    cache_block = pl.BlockSpec((together, CACHE, HEAD_DIM), lambda b: (b, 0, 0))

    height = block // RANK * NX * MOST + 8
    packed = call(
        pack_kernel,
        "pack",
        shape((peers, height, RANK)),
        out_grad,
        merge_up,
        scratch=[((peers, height, RANK), F32)],
        grid=(1,),
        limit=60,
    )
    received = lax.all_to_all(packed, ("yh", "yl", "zl", "x"), 0, 0, tiled=True)
    *turned, partial = pl.pallas_call(
        feature_kernel,
        grid=(branches // together,),
        in_specs=[
            smem,
            smem,
            smem,
            whole((count, 1)),
            whole((branches, TREE)),
            row_block,
            whole((count, HEAD_DIM)),
            whole((count, HEAD_DIM)),
            cache_block,
            cache_block,
            row_block,
            row_block,
            whole((3, width)),
            whole((width, 3 * RANK)),
        ],
        out_specs=[pl.BlockSpec(memory_space=pltpu.HBM)] * NX + [whole((count, 4 * RANK))],
        out_shape=[shape((3, block, count))] * NX + [shape((count, 4 * RANK), F32)],
        scratch_shapes=[
            pltpu.VMEM((count, count), F32),
            pltpu.VMEM((3, count, width), BF),
            pltpu.VMEM((count, RANK), F32),
            pltpu.VMEM((NX, 3, block, count), BF),
            pltpu.SemaphoreType.DMA((NX,)),
        ],
        compiler_params=params(60),
        cost_estimate=pl.CostEstimate(
            flops=400_000_000, bytes_accessed=8_000_000, transcendentals=600_000
        ),
        name="features",
    )(
        place,
        cache_lengths,
        accepted_counts,
        dest_map,
        parents,
        queries,
        tree_keys,
        tree_values,
        cache_keys,
        cache_values,
        low_hidden,
        mid_hidden,
        norm_gains,
        merge_down,
    )
    for k in range(1, NX):
        turned[k] = lax.ppermute(turned[k], "x", [(i, (i + SHIFTS[k]) % NX) for i in range(NX)])
    base, chosen = call(
        ready_kernel, "ready", [shape((count, 4 * RANK)), shape((count, peers * 8))], partial
    )
    sent = call(pick_kernel, "pick", shape((count, 5 * RANK)), received, base, chosen)
    share = count // (nzh * nc)
    parts = lax.all_to_all(sent.reshape(nzh * nc, share, 5 * RANK), ("zh", "c"), 0, 0, tiled=True)
    merged = call(
        merge_kernel,
        "merge",
        shape((NX * nzh * nc, share, 3 * RANK)),
        parts,
        unread=turned[1:],
    )
    merged = lax.all_to_all(merged, ("x", "zh", "c"), 0, 0, tiled=True)
    merged = merged.reshape(NX, count, 3 * RANK)
    slots = call(
        unpack_kernel,
        "unpack",
        shape((block // RANK * peers * NX * MOST + NX * 3 * block, RANK)),
        received,
        *turned,
        scratch=[((peers * NX * MOST, RANK), F32)],
    )
    grads = call(grads_kernel, "grads", shape((block, 4 * RANK)), place, slots, merged)
    piece = block // (nzl * nyl * nyh)
    grads = lax.all_to_all(
        grads.reshape(nzl * nyl * nyh, piece, 4 * RANK), ("zl", "yl", "yh"), 0, 0, tiled=True
    )
    grads = call(sum_kernel, "total", shape((nyh, piece, 4 * RANK)), grads)
    rows = nyh * piece
    grads = lax.all_to_all(grads, "yh", 0, 0, tiled=True).reshape(rows, 4 * RANK)
    near = nzl * nyl
    grads = jnp.broadcast_to(grads[None], (near * NX, rows, 4 * RANK))
    grads = lax.all_to_all(grads, ("zl", "yl", "x"), 0, 0, tiled=True)
    grads = grads.reshape(nzl, nyl, NX, rows, 4 * RANK)
    return pl.pallas_call(
        final_kernel,
        in_specs=[pl.BlockSpec(memory_space=pltpu.VMEM)],
        out_specs=[pl.BlockSpec(memory_space=pl.ANY)] * 2,
        out_shape=[shape((width, 3 * RANK), F32), shape((RANK, width), F32)],
        scratch_shapes=[
            pltpu.VMEM((width, 3 * RANK), F32),
            pltpu.VMEM((RANK, width), F32),
            pltpu.SemaphoreType.DMA((2, NX)),
        ],
        compiler_params=params(),
        name="final",
    )(grads)


def solution(mesh):
    fine = Mesh(mesh.devices.reshape(4, 2, 2, NX, 4, 2), ("yh", "yl", "zl", "x", "zh", "c"))
    dp, head = ("yh", "yl", "zl", "x"), ("zh", "c")
    placed = (
        P(dp, head),
        P(dp, head),
        P(dp, head),
        P(dp, None, head),
        P(dp, None, head),
        P(dp, None),
        P(dp),
        P(dp),
        P(dp, None),
        P(dp, head),
        P(dp, head),
        P(None, head),
        P(head, None),
        P(None, head),
        P(dp, head),
    )
    return jax.shard_map(
        body,
        mesh=fine,
        in_specs=placed,
        out_specs=(P(head, None), P(None, head)),
        check_vma=False,
    )
```
